32 devices in a mesh: atom: 8 (over z, x), energy: 4 (over y, core).
Axes of the slice: x: 2, y: 2, z: 4, core: 2. Of those that a mesh axis runs over, the one named last changes fastest.
Arguments:
- bare_green: bfloat16 [2, 12, 12, 32, 512], P(None, None, None, 'atom', 'energy'), may hold values from -6 to 6
- coupling_grad: bfloat16 [8, 12, 12, 32], P(None, None, None, 'atom'), may hold values from -1.75 to 1.75
- neighbours: int32 [32, 8], P('atom'), may hold values from 0 to 31, as said below
- shifts: int32 [32], replicated, may hold values from 1 to 4
- strength: float32 [32], replicated, may hold values from 5e-05 to 0.0005
- occupation: float32 [32], replicated, may hold values from 0.1 to 4
Outputs:
- green: bfloat16 [2, 12, 12, 32, 512], P(None, None, None, 'atom', 'energy')
The draws below stay inside these ranges and needn't reach their ends.
Inputs may be any that keep to these rules, and one draw needn't show every extreme that they name: Each atom's 8 neighbours differ from it by 1 to 4 in index (not necessarily distinct); in every row one lies exactly 4 away.
All inputs are finite; a program needn't handle non-finite values.
Results may differ from the reference program's by a relative error of at most 0.0071.
Values may be sent and summed in bfloat16 or wider, within the bound.
No kernel may reach another device: no remote copies, remote signals or barrier semaphores. Data moves between devices by JAX's collectives and lax.ppermute only.
A program may use at most 64 MiB of HBM per device.

```python
import math
import jax
import jax.numpy as jnp
from jax import lax

ORB = 12
NB = 8
NW = 32
WIDTH = 4
ITERS = 1
E_DEV = 128
ATOMS = 32
ENERGIES = 512


def draw_neighbours(key, part):
    key_one, key_two, key_three = jax.random.split(jax.random.fold_in(key, 17), 3)
    magnitudes = jax.random.randint(key_one, (ATOMS, NB), 1, WIDTH + 1)
    slot_pick = jax.random.randint(key_two, (ATOMS, 1), 0, NB)
    slot_index = jnp.arange(NB, dtype=jnp.int32)[None, :]
    magnitudes = jnp.where(slot_index == slot_pick, WIDTH, magnitudes)
    sign_pick = jnp.where(jax.random.randint(key_three, (ATOMS, NB), 0, 2) == 0, -1, 1)
    own_atom = jnp.arange(ATOMS, dtype=jnp.int32)[:, None]
    forward = own_atom + sign_pick * magnitudes
    outside = (forward < 0) | (forward >= ATOMS)
    return jnp.where(outside, own_atom - sign_pick * magnitudes, forward).astype(jnp.int32)


def draw_shifts(key, part):
    key_one, key_two, key_three = jax.random.split(jax.random.fold_in(key, 29), 3)
    values = jax.random.randint(key_one, (NW,), 1, WIDTH + 1)
    top_slot = jax.random.randint(key_two, (), 0, NW)
    low_slot = (top_slot + 1 + jax.random.randint(key_three, (), 0, NW - 1)) % NW
    slot_index = jnp.arange(NW, dtype=jnp.int32)
    values = jnp.where(slot_index == top_slot, WIDTH, values)
    return jnp.where(slot_index == low_slot, 1, values).astype(jnp.int32)


def block_levels(own_key, shape, cuts, least, largest):
    gain, own = 1.0, jax.random.fold_in(own_key, 6)
    for position, shards_of in cuts:
        steps = jnp.exp(jax.random.uniform(jax.random.fold_in(own, position), (shards_of,), jnp.float32, least / len(cuts), largest / len(cuts)))
        gain = gain * jnp.repeat(steps, shape[position] // shards_of).reshape([-1 if axis == position else 1 for axis in range(len(shape))])
    return gain


def bell_draw(rng, extent, scale, bound, cuts=(), kind=jnp.bfloat16):
    values = scale * jax.random.normal(rng, extent, jnp.float32)
    if cuts:
        values = values * block_levels(rng, extent, cuts, -0.22, 0.18)
    return jnp.clip(values, -bound, bound).astype(kind)


def setup_inputs(seed: int = 0) -> dict:
    arg_keys = jax.random.split(jax.random.key(seed), 7)
    bare_green = bell_draw(arg_keys[0], (2, ORB, ORB, ATOMS, ENERGIES), 1.0, 6.0, ((3, 8), (4, 4)))
    coupling_grad = bell_draw(arg_keys[1], (NB, ORB, ORB, ATOMS), ORB ** -0.5, 1.75, ((3, 8),))
    neighbours = draw_neighbours(jax.random.fold_in(arg_keys[6], 71), 0)
    shifts = draw_shifts(jax.random.fold_in(arg_keys[6], 71), 0)
    strength = jnp.clip(jnp.exp(jax.random.uniform(arg_keys[4], (NW,), jnp.float32, math.log(4.999999873689376e-05), math.log(0.0005))), 4.999999873689376e-05, 0.0005)
    occupation = jnp.clip(jnp.exp(jax.random.uniform(arg_keys[5], (NW,), jnp.float32, math.log(0.1), math.log(4.0))), 0.1, 4.0)
    return {"bare_green": bare_green, "coupling_grad": coupling_grad, "neighbours": neighbours, "shifts": shifts, "strength": strength, "occupation": occupation}


def coefficients(shifts, strength, occupation):
    offsets = jnp.arange(2 * WIDTH + 1, dtype=jnp.int32) - WIDTH
    lower_hit = offsets[:, None] == -shifts[None, :]
    upper_hit = offsets[:, None] == shifts[None, :]
    weights = jnp.where(lower_hit, (strength * occupation)[None, :], jnp.zeros((), jnp.float32))
    weights = weights + jnp.where(upper_hit, (strength * (occupation + 1.0))[None, :], jnp.zeros((), jnp.float32))
    return jnp.sum(weights, axis=1).astype(jnp.bfloat16)


def band_matrix(offset_weights, energy_count):
    row_index = jnp.arange(energy_count + 2 * WIDTH, dtype=jnp.int32)[:, None]
    col_index = jnp.arange(energy_count, dtype=jnp.int32)[None, :]
    gap_index = row_index - col_index - WIDTH
    offsets = jnp.arange(2 * WIDTH + 1, dtype=jnp.int32) - WIDTH
    pick_mask = gap_index[None, :, :] == offsets[:, None, None]
    table = jnp.where(pick_mask, offset_weights.astype(jnp.float32)[:, None, None], jnp.zeros((), jnp.float32))
    return jnp.sum(table, axis=0).astype(jnp.bfloat16)


def complex_product(factor_left, factor_right):
    left_real = factor_left[0].astype(jnp.float32)
    left_imag = factor_left[1].astype(jnp.float32)
    right_real = factor_right[0].astype(jnp.float32)
    right_imag = factor_right[1].astype(jnp.float32)
    real_part = jnp.einsum('ikae,kjae->ijae', left_real, right_real) - jnp.einsum('ikae,kjae->ijae', left_imag, right_imag)
    imag_part = jnp.einsum('ikae,kjae->ijae', left_real, right_imag) + jnp.einsum('ikae,kjae->ijae', left_imag, right_real)
    return jnp.stack([real_part, imag_part])


def sandwich(phonon_sum, index_row, grad_atom):
    picked = jnp.take(phonon_sum, index_row, axis=3)
    half_product = jnp.einsum('nik,rklne->rilne', grad_atom.astype(jnp.float32), picked.astype(jnp.float32)).astype(jnp.bfloat16)
    return jnp.einsum('rilne,njl->rije', half_product.astype(jnp.float32), grad_atom.astype(jnp.float32))


def energy_slab(green_now, block_index):
    start_index = (block_index * E_DEV).astype(jnp.int32)
    middle = lax.dynamic_slice_in_dim(green_now, start_index, E_DEV, 4)
    below_rim = lax.dynamic_slice_in_dim(green_now, jnp.maximum(start_index - WIDTH, 0).astype(jnp.int32), WIDTH, 4)
    above_rim = lax.dynamic_slice_in_dim(green_now, jnp.minimum(start_index + E_DEV, ENERGIES - WIDTH).astype(jnp.int32), WIDTH, 4)
    below_rim = jnp.where(block_index > 0, below_rim, jnp.zeros_like(below_rim))
    above_rim = jnp.where(block_index < ENERGIES // E_DEV - 1, above_rim, jnp.zeros_like(above_rim))
    return jnp.concatenate([below_rim, middle, above_rim], axis=4)


def reference(bare_green, coupling_grad, neighbours, shifts, strength, occupation):
    offset_weights = coefficients(shifts, strength, occupation)
    band_table = band_matrix(offset_weights, E_DEV)
    bond_grads = jnp.moveaxis(coupling_grad, 3, 0)
    green_now = bare_green
    for iteration in range(ITERS):
        def one_block(block_index, result):
            slab_values = energy_slab(green_now, block_index)
            flat_slab = slab_values.reshape(-1, E_DEV + 2 * WIDTH)
            phonon_sum = jnp.dot(flat_slab, band_table, preferred_element_type=jnp.float32).astype(jnp.bfloat16)
            phonon_sum = phonon_sum.reshape(2, ORB, ORB, ATOMS, E_DEV)

            def per_atom(atom_item):
                return sandwich(phonon_sum, atom_item[0], atom_item[1])

            self_energy = lax.map(per_atom, (neighbours, bond_grads))
            self_energy = jnp.moveaxis(self_energy, 0, 3).astype(jnp.bfloat16)
            start_index = (block_index * E_DEV).astype(jnp.int32)
            free_block = lax.dynamic_slice_in_dim(bare_green, start_index, E_DEV, 4)
            left_product = complex_product(free_block, self_energy).astype(jnp.bfloat16)
            updated_block = (free_block.astype(jnp.float32) + complex_product(left_product, free_block)).astype(jnp.bfloat16)
            return lax.dynamic_update_slice_in_dim(result, updated_block, start_index, 4)

        green_now = lax.fori_loop(0, ENERGIES // E_DEV, one_block, jnp.zeros_like(bare_green))
    return green_now
```

```python
import functools
import math
import jax
import jax.numpy as jnp
from jax import lax
from jax.experimental import pallas as pl
from jax.experimental.pallas import tpu as pltpu
from jax.sharding import PartitionSpec as P

WIDTH = 4
EDGE = 2 * WIDTH
LANES = 128
F32 = jnp.float32
BF16 = jnp.bfloat16


def iota(shape, axis):
    return lax.broadcasted_iota(jnp.int32, shape, axis)


def dot(a, b, dims=((1,), (0,))):
    return lax.dot_general(a, b, (dims, ((), ())), preferred_element_type=F32)


def steps_below(x, step, most):
    return sum((x >= step * m).astype(jnp.int32) for m in range(1, most))


def pack_kernel(g_ref, edge_ref):
    energies = g_ref.shape[2]
    row = iota((EDGE, energies), 0)
    lane = iota((EDGE, energies), 1)
    want = jnp.where(row < WIDTH, row, row + energies - EDGE)
    pick = (lane == want).astype(F32).astype(BF16)
    parts = [dot(pick, g_ref[r], ((1,), (1,))) for r in range(2)]
    edge_ref[...] = jnp.concatenate(parts, axis=0).astype(BF16)


def band_weights(sh_ref, st_ref, oc_ref):
    shifts = sh_ref[...]
    emit = st_ref[...] * oc_ref[...]
    absorb = st_ref[...] * (oc_ref[...] + 1.0)
    zero = jnp.zeros_like(emit)
    weights = []
    for o in range(-WIDTH, WIDTH + 1):
        both = jnp.where(shifts == -o, emit, zero) + jnp.where(shifts == o, absorb, zero)
        weights.append(jnp.sum(both, axis=1, keepdims=True))
    return weights


def banded(weights, gap, keep=None):
    table = jnp.zeros(gap.shape, F32)
    for o in range(-WIDTH, WIDTH + 1):
        hit = gap == o
        if keep is not None:
            hit = hit & keep
        table = jnp.where(hit, weights[o + WIDTH], table)
    return table.astype(BF16)


def weights_kernel(orb, c_ref, nbr_ref, g_ref, sh_ref, st_ref, oc_ref,
                   wl_ref, wo_ref, wh_ref, s_ref, band_ref, rim_ref, t1_ref, t2_ref):
    atoms, bonds = nbr_ref.shape
    energies = g_ref.shape[2]
    span = orb * atoms
    cols = t1_ref.shape[3]
    tiles = cols // LANES
    period = t2_ref.shape[4]
    here = lax.axis_index("atom")
    place = lax.axis_index("energy")
    last = lax.axis_size("energy") - 1

    weights = band_weights(sh_ref, st_ref, oc_ref)
    band_ref[...] = banded(weights, iota((energies, energies), 0) - iota((energies, energies), 1))
    rim = (2 * EDGE, energies)
    row = iota(rim, 0)
    spot = row & (EDGE - 1)
    lane = iota(rim, 1)
    low_part = spot < WIDTH
    keep = jnp.where(low_part, jnp.where(place < last, 1, 0), jnp.where(place > 0, 1, 0)) > 0
    gap = jnp.where(low_part, energies + spot, spot - EDGE) - lane
    for r in range(2):
        rim_ref[r] = banded(weights, gap, keep & ((row >= EDGE) == (r == 1)))

    c = c_ref[...]
    krow, klane = iota((orb, cols), 0), iota((orb, cols), 1)
    spread = ((klane >= krow * span) & (klane < (krow + 1) * span)).astype(F32).astype(BF16)
    left = dot(c, spread).reshape(bonds * orb * atoms // 8, 8, cols)
    turned = pltpu.roll(left, atoms, 1)
    upper = iota(left.shape, 1) < atoms
    first = jnp.where(upper, left, turned)
    second = jnp.where(upper, turned, left)
    both = jnp.stack([first, second], axis=1).reshape(bonds, orb, 8, cols)
    t1_ref[...] = jnp.concatenate([both, both], axis=2).astype(BF16)

    lrow, llane = iota((orb, period), 0), iota((orb, period), 1)
    inner = llane - span * steps_below(llane, span, period // span)
    spread = ((inner >= lrow * atoms) & (inner < (lrow + 1) * atoms)).astype(F32).astype(BF16)
    right = dot(c, spread).reshape(bonds, span // 16, 16, period)
    own = iota((16, period), 0) & (atoms - 1)
    other = iota((16, period), 1) & (atoms - 1)
    for n in range(bonds):
        near = jnp.zeros((16, period), jnp.int32)
        for a in range(atoms):
            near = jnp.where(own == a, nbr_ref[a, n], near)
        for s in range(3):
            mask = near == other + (here + (s - 1)) * atoms
            t2_ref[s, n] = jnp.where(mask[None], right[n], 0.0).astype(BF16)

    for t in range(tiles):
        at = slice(t * LANES, (t + 1) * LANES)
        start = (t * LANES) % period
        cut = slice(start, start + LANES)

        def body(i, carry):
            x = t1_ref[:, i, :, at]
            for s, out in enumerate((wl_ref, wo_ref, wh_ref)):
                for q in range(span // 16):
                    total = x[0] * t2_ref[s, 0, q, :, cut]
                    for n in range(1, bonds):
                        total = total + x[n] * t2_ref[s, n, q, :, cut]
                    out[i, q * 16:(q + 1) * 16, at] = total
            return carry

        lax.fori_loop(0, orb, body, 0)

    s_ref[...] = slab_product(wo_ref, g_ref)


def slab_product(w_ref, g_ref):
    rows = g_ref.shape[1]
    w = w_ref[...].reshape(rows, w_ref.shape[2])[:, :rows]
    return dot(w, jnp.concatenate([g_ref[0], g_ref[1]], axis=1))


def rim_product(w_ref, f_ref):
    rows = f_ref.shape[1]
    w = w_ref[...].reshape(rows, w_ref.shape[2])[:, :rows]
    return dot(w, f_ref[...], ((1,), (1,)))


def doubled(x, orb, atoms):
    pairs = x.reshape(orb * orb * atoms // 8, 8, x.shape[1])
    turned = pltpu.roll(pairs, atoms, 1)
    upper = iota(pairs.shape, 1) < atoms
    first = jnp.where(upper, pairs, turned)
    second = jnp.where(upper, turned, pairs)
    return jnp.stack([first, second], axis=1).reshape(orb, orb, 8, x.shape[1])


def final_kernel(orb, atoms, g_ref, gl_ref, gh_ref, f_ref, fl_ref, fh_ref, wl_ref, wo_ref, wh_ref,
                 s_ref, band_ref, rim_ref, out_ref, gn_ref, gd_ref, sn_ref, ld_ref):
    rows = g_ref.shape[1]
    energies = g_ref.shape[2]
    groups = orb * atoms // 8

    def put(ref, c, x):
        ref[c] = x.reshape(orb, groups, 8, energies)

    gr = g_ref[0].astype(F32)
    gi = g_ref[1].astype(F32)
    for c, x in enumerate((gr, gi, gr + gi)):
        put(gn_ref, c, x)
        gd_ref[c] = doubled(x, orb, atoms)

    total = s_ref[...] + slab_product(wl_ref, gl_ref) + slab_product(wh_ref, gh_ref)
    rim = rim_product(wo_ref, f_ref) + rim_product(wl_ref, fl_ref) + rim_product(wh_ref, fh_ref)
    rim = rim.astype(BF16)
    parts = []
    for r in range(2):
        body = total[:, r * energies:(r + 1) * energies].astype(BF16)
        parts.append(dot(body, band_ref[...]) + dot(rim, rim_ref[r]))
    for c, x in enumerate((parts[0], parts[1], parts[0] + parts[1])):
        put(sn_ref, c, x)

    def product(left, right_ref, acc):
        for k in range(orb):
            for c in range(3):
                right = right_ref[c, k]
                for d in range(2):
                    term = left(c, d, k)[None] * right
                    acc[c][d] = term if acc[c][d] is None else acc[c][d] + term
        return acc

    def pair(p, carry):
        m = product(lambda c, d, k: gd_ref[c, 2 * p + d, k], sn_ref, [[None, None] for _ in range(3)])
        upper = iota((groups, 8, energies), 1) < atoms
        for d in range(2):
            lr = m[0][d] - m[1][d]
            li = m[2][d] - (m[0][d] + m[1][d])
            for c, x in enumerate((lr, li, lr + li)):
                turned = pltpu.roll(x, atoms, 1)
                first = jnp.where(upper, x, turned)
                second = jnp.where(upper, turned, x)
                ld_ref[c, d] = jnp.stack([first, second], axis=1).reshape(orb, 8, energies)
        m = product(lambda c, d, k: ld_ref[c, d, k], gn_ref, [[None, None] for _ in range(3)])
        for d in range(2):
            i = 2 * p + d
            ur = gn_ref[0, i] + (m[0][d] - m[1][d])
            ui = gn_ref[1, i] + (m[2][d] - (m[0][d] + m[1][d]))
            out_ref[0, i] = ur.reshape(orb * atoms, energies).astype(BF16)
            out_ref[1, i] = ui.reshape(orb * atoms, energies).astype(BF16)
        return carry

    lax.fori_loop(0, orb // 2, pair, 0)


def ring(value, axis, step):
    count = lax.axis_size(axis)
    return lax.ppermute(value, axis, [(i, (i + step) % count) for i in range(count)])


def per_device(bare_green, coupling_grad, neighbours, shifts, strength, occupation):
    _, orb, _, atoms, energies = bare_green.shape
    bonds = coupling_grad.shape[0]
    rows = orb * orb * atoms
    span = orb * atoms
    cols = -(-rows // LANES) * LANES
    period = span * LANES // math.gcd(span, LANES)
    vmem = pl.BlockSpec(memory_space=pltpu.VMEM)
    smem = pl.BlockSpec(memory_space=pltpu.SMEM)
    big = pltpu.CompilerParams(vmem_limit_bytes=48 * 1024 * 1024)

    green = bare_green.reshape(2, rows, energies)
    from_low = ring(green, "atom", 1)
    from_high = ring(green, "atom", -1)

    edge = pl.pallas_call(
        pack_kernel,
        out_shape=jax.ShapeDtypeStruct((2 * EDGE, rows), BF16),
        in_specs=[vmem], out_specs=vmem, name="pack_edges",
    )(green)
    edge_low = ring(edge, "energy", 1)
    edge_high = ring(edge, "energy", -1)
    high_side = (jnp.arange(2 * EDGE, dtype=jnp.int32)[:, None] & WIDTH) > 0
    rim = jnp.where(high_side, edge_low, edge_high)
    rim_low = ring(rim, "atom", 1)
    rim_high = ring(rim, "atom", -1)

    grads = jnp.transpose(coupling_grad, (0, 1, 3, 2)).reshape(bonds * orb * atoms, orb)
    w_shape = jax.ShapeDtypeStruct((orb, span, cols), BF16)
    w_low, w_own, w_high, partial_sum, band, rim_band = pl.pallas_call(
        functools.partial(weights_kernel, orb),
        out_shape=[
            w_shape, w_shape, w_shape,
            jax.ShapeDtypeStruct((rows, 2 * energies), F32),
            jax.ShapeDtypeStruct((energies, energies), BF16),
            jax.ShapeDtypeStruct((2, 2 * EDGE, energies), BF16),
        ],
        in_specs=[vmem, smem, vmem, vmem, vmem, vmem], out_specs=[vmem] * 6,
        scratch_shapes=[
            pltpu.VMEM((bonds, orb, 16, cols), BF16),
            pltpu.VMEM((3, bonds, span // 16, 16, period), BF16),
        ],
        compiler_params=big, name="weights",
    )(grads, neighbours, green, shifts[None], strength[None], occupation[None])

    full = (3, orb, span // 8, 8, energies)
    result = pl.pallas_call(
        functools.partial(final_kernel, orb, atoms),
        out_shape=jax.ShapeDtypeStruct((2, orb, span, energies), BF16),
        in_specs=[vmem] * 12, out_specs=vmem,
        scratch_shapes=[
            pltpu.VMEM(full, F32),
            pltpu.VMEM((3, orb, orb, 8, energies), F32),
            pltpu.VMEM(full, F32),
            pltpu.VMEM((3, 2, orb, 8, energies), F32),
        ],
        compiler_params=big, name="green_update",
    )(green, from_low, from_high, rim, rim_low, rim_high, w_low, w_own, w_high, partial_sum, band, rim_band)
    return result.reshape(bare_green.shape)


def solution(mesh):
    placed = (
        P(None, None, None, "atom", "energy"),
        P(None, None, None, "atom"),
        P("atom", None),
        P(),
        P(),
        P(),
    )
    return jax.shard_map(
        per_device,
        mesh=mesh,
        in_specs=placed,
        out_specs=P(None, None, None, "atom", "energy"),
        check_vma=False,
    )
```

```python
import functools
import math
import jax
import jax.numpy as jnp
from jax import lax
from jax.experimental import pallas as pl
from jax.experimental.pallas import tpu as pltpu
from jax.sharding import PartitionSpec as P

WIDTH = 4
EDGE = 2 * WIDTH
LANES = 128
F32 = jnp.float32
BF16 = jnp.bfloat16


def iota(shape, axis):
    return lax.broadcasted_iota(jnp.int32, shape, axis)


def dot(a, b, dims=((1,), (0,))):
    return lax.dot_general(a, b, (dims, ((), ())), preferred_element_type=F32)


def steps_below(x, step, most):
    return sum((x >= step * m).astype(jnp.int32) for m in range(1, most))


def pack_kernel(g_ref, edge_ref):
    energies = g_ref.shape[2]
    row = iota((EDGE, energies), 0)
    lane = iota((EDGE, energies), 1)
    want = jnp.where(row < WIDTH, row, row + energies - EDGE)
    pick = (lane == want).astype(F32).astype(BF16)
    parts = [dot(pick, g_ref[r], ((1,), (1,))) for r in range(2)]
    edge_ref[...] = jnp.concatenate(parts, axis=0).astype(BF16)


def rim_kernel(low_ref, high_ref, after_ref, rim_ref):
    below = (iota(rim_ref.shape, 0) & WIDTH) == 0
    low, high = low_ref[...].astype(F32), high_ref[...].astype(F32)
    rim_ref[...] = jnp.where(below, high, low).astype(BF16)


def band_weights(sh_ref, st_ref, oc_ref):
    shifts = sh_ref[...]
    emit = st_ref[...] * oc_ref[...]
    absorb = st_ref[...] * (oc_ref[...] + 1.0)
    zero = jnp.zeros_like(emit)
    weights = []
    for o in range(-WIDTH, WIDTH + 1):
        both = jnp.where(shifts == -o, emit, zero) + jnp.where(shifts == o, absorb, zero)
        weights.append(jnp.sum(both, axis=1, keepdims=True))
    return weights


def banded(weights, gap, keep=None):
    table = jnp.zeros(gap.shape, F32)
    for o in range(-WIDTH, WIDTH + 1):
        hit = gap == o
        if keep is not None:
            hit = hit & keep
        table = jnp.where(hit, weights[o + WIDTH], table)
    return table.astype(BF16)


def weights_kernel(orb, c_ref, nbr_ref, g_ref, sh_ref, st_ref, oc_ref,
                   wl_ref, wo_ref, wh_ref, s_ref, band_ref, rim_ref, t1_ref, t2_ref):
    atoms, bonds = nbr_ref.shape
    energies = g_ref.shape[2]
    span = orb * atoms
    cols = t1_ref.shape[3]
    tiles = cols // LANES
    period = t2_ref.shape[4]
    here = lax.axis_index("atom")
    place = lax.axis_index("energy")
    last = lax.axis_size("energy") - 1

    weights = band_weights(sh_ref, st_ref, oc_ref)
    band_ref[...] = banded(weights, iota((energies, energies), 0) - iota((energies, energies), 1))
    rim = (2 * EDGE, energies)
    row = iota(rim, 0)
    spot = row & (EDGE - 1)
    lane = iota(rim, 1)
    low_part = spot < WIDTH
    keep = jnp.where(low_part, jnp.where(place < last, 1, 0), jnp.where(place > 0, 1, 0)) > 0
    gap = jnp.where(low_part, energies + spot, spot - EDGE) - lane
    for r in range(2):
        rim_ref[r] = banded(weights, gap, keep & ((row >= EDGE) == (r == 1)))

    c = c_ref[...]
    krow, klane = iota((orb, cols), 0), iota((orb, cols), 1)
    spread = ((klane >= krow * span) & (klane < (krow + 1) * span)).astype(F32).astype(BF16)
    left = dot(c, spread).reshape(bonds * orb * atoms // 8, 8, cols)
    turned = pltpu.roll(left, atoms, 1)
    upper = iota(left.shape, 1) < atoms
    first = jnp.where(upper, left, turned)
    second = jnp.where(upper, turned, left)
    both = jnp.stack([first, second], axis=1).reshape(bonds, orb, 8, cols)
    t1_ref[...] = jnp.concatenate([both, both], axis=2).astype(BF16)

    lrow, llane = iota((orb, period), 0), iota((orb, period), 1)
    inner = llane - span * steps_below(llane, span, period // span)
    spread = ((inner >= lrow * atoms) & (inner < (lrow + 1) * atoms)).astype(F32).astype(BF16)
    right = dot(c, spread).reshape(bonds, span // 16, 16, period)
    odd = here & 1
    base = (here + 1 - 2 * odd, here, here - 1 + 2 * odd)
    own = iota((16, period), 0) & (atoms - 1)
    other = iota((16, period), 1) & (atoms - 1)
    for n in range(bonds):
        near = jnp.zeros((16, period), jnp.int32)
        for a in range(atoms):
            near = jnp.where(own == a, nbr_ref[a, n], near)
        for s in range(3):
            mask = near == other + base[s] * atoms
            t2_ref[s, n] = jnp.where(mask[None], right[n], 0.0).astype(BF16)

    for t in range(tiles):
        at = slice(t * LANES, (t + 1) * LANES)
        start = (t * LANES) % period
        cut = slice(start, start + LANES)

        def body(i, carry):
            x = t1_ref[:, i, :, at]
            for s, out in enumerate((wl_ref, wo_ref, wh_ref)):
                for q in range(span // 16):
                    total = x[0] * t2_ref[s, 0, q, :, cut]
                    for n in range(1, bonds):
                        total = total + x[n] * t2_ref[s, n, q, :, cut]
                    out[i, q * 16:(q + 1) * 16, at] = total
            return carry

        lax.fori_loop(0, orb, body, 0)

    s_ref[...] = slab_product(wo_ref, g_ref.at[0], g_ref.at[1])


def slab_product(w_ref, *parts):
    rows = parts[0].shape[0]
    w = w_ref[...].reshape(rows, w_ref.shape[2])[:, :rows]
    return dot(w, jnp.concatenate([x[...] for x in parts], axis=1))


def rim_product(w_ref, f_ref):
    rows = f_ref.shape[1]
    w = w_ref[...].reshape(rows, w_ref.shape[2])[:, :rows]
    return dot(w, f_ref[...], ((1,), (1,)))


def doubled(x, orb, atoms):
    pairs = x.reshape(orb * orb * atoms // 8, 8, x.shape[1])
    turned = pltpu.roll(pairs, atoms, 1)
    upper = iota(pairs.shape, 1) < atoms
    first = jnp.where(upper, pairs, turned)
    second = jnp.where(upper, turned, pairs)
    return jnp.stack([first, second], axis=1).reshape(orb, orb, 8, x.shape[1])


def final_kernel(orb, atoms, g_ref, b_ref, a_ref, f_ref, fl_ref, fh_ref, wl_ref, wo_ref, wh_ref,
                 s_ref, band_ref, rim_ref, out_ref, gn_ref, gd_ref, sn_ref, ld_ref):
    rows = g_ref.shape[1]
    energies = g_ref.shape[2]
    groups = orb * atoms // 8

    def put(ref, c, x):
        ref[c] = x.reshape(orb, groups, 8, energies)

    gr = g_ref[0].astype(F32)
    gi = g_ref[1].astype(F32)
    for c, x in enumerate((gr, gi, gr + gi)):
        put(gn_ref, c, x)
        gd_ref[c] = doubled(x, orb, atoms)

    total = s_ref[...] + slab_product(wl_ref, a_ref.at[0], a_ref.at[1]) + slab_product(wh_ref, b_ref.at[0], b_ref.at[1])
    rim = rim_product(wo_ref, f_ref) + rim_product(wl_ref, fl_ref) + rim_product(wh_ref, fh_ref)
    rim = rim.astype(BF16)
    parts = []
    for r in range(2):
        body = total[:, r * energies:(r + 1) * energies].astype(BF16)
        parts.append(dot(body, band_ref[...]) + dot(rim, rim_ref[r]))
    for c, x in enumerate((parts[0], parts[1], parts[0] + parts[1])):
        put(sn_ref, c, x)

    def product(left, right_ref, acc):
        for k in range(orb):
            for c in range(3):
                right = right_ref[c, k]
                for d in range(2):
                    term = left(c, d, k)[None] * right
                    acc[c][d] = term if acc[c][d] is None else acc[c][d] + term
        return acc

    def pair(p, carry):
        m = product(lambda c, d, k: gd_ref[c, 2 * p + d, k], sn_ref, [[None, None] for _ in range(3)])
        upper = iota((groups, 8, energies), 1) < atoms
        for d in range(2):
            lr = m[0][d] - m[1][d]
            li = m[2][d] - (m[0][d] + m[1][d])
            for c, x in enumerate((lr, li, lr + li)):
                turned = pltpu.roll(x, atoms, 1)
                first = jnp.where(upper, x, turned)
                second = jnp.where(upper, turned, x)
                ld_ref[c, d] = jnp.stack([first, second], axis=1).reshape(orb, 8, energies)
        m = product(lambda c, d, k: ld_ref[c, d, k], gn_ref, [[None, None] for _ in range(3)])
        for d in range(2):
            i = 2 * p + d
            ur = gn_ref[0, i] + (m[0][d] - m[1][d])
            ui = gn_ref[1, i] + (m[2][d] - (m[0][d] + m[1][d]))
            out_ref[0, i] = ur.reshape(orb * atoms, energies).astype(BF16)
            out_ref[1, i] = ui.reshape(orb * atoms, energies).astype(BF16)
        return carry

    lax.fori_loop(0, orb // 2, pair, 0)


def move(value, axis, target):
    count = lax.axis_size(axis)
    return lax.ppermute(value, axis, [(i, target(i) % count) for i in range(count)])


def ring(value, axis, step):
    return move(value, axis, lambda i: i + step)


def pair(i):
    return i ^ 1


def relay(i, count):
    if i & 1:
        return i - 2 if i > 1 else 0
    return i + 2 if i + 2 < count else count - 1


def move_far(value):
    atoms, energies = lax.axis_size("atom"), lax.axis_size("energy")
    moves = []
    for a in range(atoms):
        b = a + 1 if a & 1 else a - 1
        for e in range(energies):
            target = (b, e) if 0 <= b < atoms else (a, (e ^ 1) % energies)
            moves.append((a * energies + e, target[0] * energies + target[1]))
    return lax.ppermute(value, ("atom", "energy"), moves)


def per_device(bare_green, coupling_grad, neighbours, shifts, strength, occupation):
    _, orb, _, atoms, energies = bare_green.shape
    bonds = coupling_grad.shape[0]
    rows = orb * orb * atoms
    span = orb * atoms
    cols = -(-rows // LANES) * LANES
    period = span * LANES // math.gcd(span, LANES)
    vmem = pl.BlockSpec(memory_space=pltpu.VMEM)
    smem = pl.BlockSpec(memory_space=pltpu.SMEM)
    big = pltpu.CompilerParams(vmem_limit_bytes=20 * 1024 * 1024)

    green = bare_green.reshape(2, rows, energies)
    far = move_far(green)
    near = move(green, "atom", pair)
    edge = pl.pallas_call(
        pack_kernel,
        out_shape=jax.ShapeDtypeStruct((2 * EDGE, rows), BF16),
        in_specs=[vmem], out_specs=vmem, compiler_params=big, name="pack_edges",
    )(green)
    grads = jnp.transpose(coupling_grad, (0, 1, 3, 2)).reshape(bonds * orb * atoms, orb)
    w_shape = jax.ShapeDtypeStruct((orb, span, cols), BF16)
    w_low, w_own, w_high, partial_sum, band, rim_band = pl.pallas_call(
        functools.partial(weights_kernel, orb),
        out_shape=[
            w_shape, w_shape, w_shape,
            jax.ShapeDtypeStruct((rows, 2 * energies), F32),
            jax.ShapeDtypeStruct((energies, energies), BF16),
            jax.ShapeDtypeStruct((2, 2 * EDGE, energies), BF16),
        ],
        in_specs=[vmem, smem, vmem, vmem, vmem, vmem], out_specs=[vmem] * 6,
        scratch_shapes=[
            pltpu.VMEM((bonds, orb, 16, cols), BF16),
            pltpu.VMEM((3, bonds, span // 16, 16, period), BF16),
        ],
        compiler_params=big, name="weights",
    )(grads, neighbours, green, shifts[None], strength[None], occupation[None])

    rim = pl.pallas_call(
        rim_kernel, out_shape=jax.ShapeDtypeStruct((2 * EDGE, rows), BF16),
        in_specs=[vmem] * 3, out_specs=vmem, compiler_params=big, name="rim",
    )(ring(edge, "energy", 1), ring(edge, "energy", -1), band)
    rim_low = move(rim, "atom", pair)
    rim_high = move_far(rim)

    full = (3, orb, span // 8, 8, energies)
    result = pl.pallas_call(
        functools.partial(final_kernel, orb, atoms),
        out_shape=jax.ShapeDtypeStruct((2, orb, span, energies), BF16),
        in_specs=[vmem] * 12, out_specs=vmem,
        scratch_shapes=[
            pltpu.VMEM(full, F32),
            pltpu.VMEM((3, orb, orb, 8, energies), F32),
            pltpu.VMEM(full, F32),
            pltpu.VMEM((3, 2, orb, 8, energies), F32),
        ],
        compiler_params=big, name="green_update",
    )(green, far, near, rim, rim_low, rim_high, w_low, w_own, w_high, partial_sum, band, rim_band)
    return result.reshape(bare_green.shape)


def solution(mesh):
    placed = (
        P(None, None, None, "atom", "energy"),
        P(None, None, None, "atom"),
        P("atom", None),
        P(),
        P(),
        P(),
    )
    return jax.shard_map(
        per_device,
        mesh=mesh,
        in_specs=placed,
        out_specs=P(None, None, None, "atom", "energy"),
        check_vma=False,
    )
```

```python
import functools
import math
import jax
import jax.numpy as jnp
from jax import lax
from jax.experimental import pallas as pl
from jax.experimental.pallas import tpu as pltpu
from jax.sharding import PartitionSpec as P

WIDTH = 4
EDGE = 2 * WIDTH
LANES = 128
F32 = jnp.float32
BF16 = jnp.bfloat16


def iota(shape, axis):
    return lax.broadcasted_iota(jnp.int32, shape, axis)


def dot(a, b, dims=((1,), (0,))):
    return lax.dot_general(a, b, (dims, ((), ())), preferred_element_type=F32)


def steps_below(x, step, most):
    return sum((x >= step * m).astype(jnp.int32) for m in range(1, most))


def pack_kernel(orb, g_hbm, c_hbm, nbr_hbm, sh_hbm, st_hbm, oc_hbm,
                edge_ref, g_ref, c_ref, near_ref, sh_ref, st_ref, oc_ref, nbr_ref, sems):
    ends = ((g_hbm, g_ref), (nbr_hbm, nbr_ref), (c_hbm, c_ref), (sh_hbm, sh_ref), (st_hbm, st_ref), (oc_hbm, oc_ref))
    copies = [pltpu.make_async_copy(source, target, sems.at[i]) for i, (source, target) in enumerate(ends)]
    for copy in copies:
        copy.start()
    copies[0].wait()
    span = g_ref.shape[1] // orb
    lane = iota((span, LANES), 1)
    for r in range(2):
        total = jnp.zeros((span, LANES), F32)
        for k in range(orb):
            x = g_ref[r, k * span:(k + 1) * span].astype(F32)
            turned = pltpu.roll(x, EDGE * k + WIDTH, 1)
            total = jnp.where((lane >= EDGE * k) & (lane < EDGE * (k + 1)), turned, total)
        edge_ref[r * span:(r + 1) * span] = total.astype(BF16)
    copies[1].wait()
    atoms, bonds = nbr_ref.shape
    own = iota(near_ref.shape[1:], 0) & (atoms - 1)
    for n in range(bonds):
        near = jnp.zeros(near_ref.shape[1:], jnp.int32)
        for a in range(atoms):
            near = jnp.where(own == a, nbr_ref[a, n], near)
        near_ref[n] = near
    for copy in copies[2:]:
        copy.wait()


def join_kernel(low_ref, high_ref, g_ref, after_ref, out_ref, rim_ref):
    rows = g_ref.shape[1]
    rim = low_ref.shape[0]
    rest = (out_ref.shape[0] - rim) // 2
    for r in range(2):
        out_ref[r * rest:(r + 1) * rest] = g_ref[r, rows - rest:]
    below = (iota(low_ref.shape, 1) & WIDTH) == 0
    low, high = low_ref[...].astype(F32), high_ref[...].astype(F32)
    halo = jnp.where(below, low, high).astype(BF16)
    out_ref[2 * rest:] = halo
    rim_ref[...] = halo


def pass_kernel(x_ref, after_ref, out_ref):
    out_ref[...] = x_ref[:, :out_ref.shape[1]]


def band_weights(sh_ref, st_ref, oc_ref):
    shifts = sh_ref[...]
    emit = st_ref[...] * oc_ref[...]
    absorb = st_ref[...] * (oc_ref[...] + 1.0)
    zero = jnp.zeros_like(emit)
    weights = []
    for o in range(-WIDTH, WIDTH + 1):
        both = jnp.where(shifts == -o, emit, zero) + jnp.where(shifts == o, absorb, zero)
        weights.append(jnp.sum(both, axis=1, keepdims=True))
    return weights


def banded(weights, gap, keep=None):
    table = jnp.zeros(gap.shape, F32)
    for o in range(-WIDTH, WIDTH + 1):
        hit = gap == o
        if keep is not None:
            hit = hit & keep
        table = jnp.where(hit, weights[o + WIDTH], table)
    return table.astype(BF16)


def factors_kernel(orb, atoms, c_ref, near_ref, sh_ref, st_ref, oc_ref, t1_ref, t2_ref, table_ref):
    bonds = near_ref.shape[0]
    energies = table_ref.shape[2]
    span = orb * atoms
    cols = t1_ref.shape[3]
    period = t2_ref.shape[4]
    here = lax.axis_index("atom")
    place = lax.axis_index("energy")
    last = lax.axis_size("energy") - 1

    weights = band_weights(sh_ref, st_ref, oc_ref)
    band = banded(weights, iota((energies, energies), 0) - iota((energies, energies), 1))
    rim = (LANES, energies)
    row = iota(rim, 0)
    spot = row & (EDGE - 1)
    below = spot < WIDTH
    keep = jnp.where(below, jnp.where(place > 0, 1, 0), jnp.where(place < last, 1, 0)) > 0
    edge = banded(weights, jnp.where(below, spot - WIDTH, spot - WIDTH + energies) - iota(rim, 1), keep)
    for k in range(orb):
        table_ref[k, :energies] = band
        table_ref[k, energies:] = jnp.where((row >= EDGE * k) & (row < EDGE * (k + 1)), edge, jnp.zeros_like(edge))

    c = c_ref[...]
    krow, klane = iota((orb, cols), 0), iota((orb, cols), 1)
    spread = ((klane >= krow * span) & (klane < (krow + 1) * span)).astype(F32).astype(BF16)
    left = dot(c, spread).reshape(bonds * orb * atoms // 8, 8, cols)
    turned = pltpu.roll(left, atoms, 1)
    upper = iota(left.shape, 1) < atoms
    first = jnp.where(upper, left, turned)
    second = jnp.where(upper, turned, left)
    both = jnp.stack([first, second], axis=1).reshape(bonds, orb, 8, cols)
    t1_ref[...] = jnp.concatenate([both, both], axis=2).astype(BF16)

    lrow, llane = iota((orb, period), 0), iota((orb, period), 1)
    inner = llane - span * steps_below(llane, span, period // span)
    spread = ((inner >= lrow * atoms) & (inner < (lrow + 1) * atoms)).astype(F32).astype(BF16)
    right = dot(c, spread).reshape(bonds, span // 16, 16, period)
    odd = here & 1
    base = (here + 1 - 2 * odd, here, here - 1 + 2 * odd)
    other = iota((16, period), 1) & (atoms - 1)
    for n in range(bonds):
        near = jnp.concatenate([near_ref[n]] * (period // LANES), axis=1)
        for s in range(3):
            mask = near == other + base[s] * atoms
            t2_ref[s, n] = jnp.where(mask[None], right[n], 0.0).astype(BF16)


def weights_kernel(orb, atoms, t1_ref, t2_ref, table_ref, g_ref, rim_ref, wl_ref, wo_ref, wh_ref, s_ref, gn_ref, gd_ref):
    bonds = t1_ref.shape[0]
    span = orb * atoms
    tiles = t1_ref.shape[3] // LANES
    period = t2_ref.shape[4]
    gr = g_ref[0].astype(F32)
    gi = g_ref[1].astype(F32)
    for c, x in enumerate((gr, gi, gr + gi)):
        gn_ref[c] = x.reshape(gn_ref.shape[1:])
        gd_ref[c] = doubled(x, orb, atoms)

    for t in range(tiles):
        at = slice(t * LANES, (t + 1) * LANES)
        start = (t * LANES) % period
        cut = slice(start, start + LANES)

        def body(i, carry):
            x = t1_ref[:, i, :, at]
            for s, out in enumerate((wl_ref, wo_ref, wh_ref)):
                for q in range(span // 16):
                    total = x[0] * t2_ref[s, 0, q, :, cut]
                    for n in range(1, bonds):
                        total = total + x[n] * t2_ref[s, n, q, :, cut]
                    out[i, q * 16:(q + 1) * 16, at] = total
            return carry

        lax.fori_loop(0, orb, body, 0)

    s_ref[...] = slab_products([wo_ref], [whole(g_ref, orb)], [rim_ref[...]], table_ref)


def rim_of(join_ref, span):
    return join_ref[join_ref.shape[0] - 2 * span:]


def whole(ref, orb):
    return [[(ref.at[0], k), (ref.at[1], k)] for k in range(orb)]


def joined(first_ref, join_ref, orb, span):
    early = first_ref.shape[1] // span
    late = orb - early
    blocks = [[(first_ref.at[0], k), (first_ref.at[1], k)] for k in range(early)]
    return blocks + [[(join_ref, k), (join_ref, late + k)] for k in range(late)]


def slab_products(w_refs, slabs, rims, table_ref):
    orb = len(slabs[0])
    span = rims[0].shape[0] // 2
    rims = jnp.concatenate(rims, axis=0)
    summed = []
    for k in range(orb):
        body = jnp.concatenate([ref[i * span:(i + 1) * span] for slab in slabs for ref, i in slab[k]], axis=0)
        summed.append(dot(jnp.concatenate([body, rims], axis=1), table_ref[k]).astype(BF16))
    total = None
    for s, w_ref in enumerate(w_refs):
        at = 2 * s * span
        right = jnp.concatenate(
            [jnp.concatenate([x[at:at + span], x[at + span:at + 2 * span]], axis=1) for x in summed], axis=0)
        rows = right.shape[0]
        w = w_ref[...].reshape(rows, w_ref.shape[2])[:, :rows]
        part = dot(w, right)
        total = part if total is None else total + part
    return total


def doubled(x, orb, atoms):
    pairs = x.reshape(orb * orb * atoms // 8, 8, x.shape[1])
    turned = pltpu.roll(pairs, atoms, 1)
    upper = iota(pairs.shape, 1) < atoms
    first = jnp.where(upper, pairs, turned)
    second = jnp.where(upper, turned, pairs)
    return jnp.stack([first, second], axis=1).reshape(orb, orb, 8, x.shape[1])


def final_kernel(orb, atoms, near_ref, rim_ref, ff_ref, fj_ref, wn_ref, wf_ref, s_ref, table_ref, gn_ref, gd_ref,
                 out_ref, sn_ref, ld_ref):
    energies = table_ref.shape[2]
    span = orb * atoms
    groups = span // 8
    slabs = [whole(near_ref, orb), joined(ff_ref, fj_ref, orb, span)]
    rims = [rim_ref[...], rim_of(fj_ref, span)]
    total = s_ref[...] + slab_products([wn_ref, wf_ref], slabs, rims, table_ref)
    re, im = total[:, :energies], total[:, energies:]
    for c, x in enumerate((re, im, re + im)):
        sn_ref[c] = x.reshape(orb, groups, 8, energies)

    def product(left, right_ref, acc):
        for k in range(orb):
            for c in range(3):
                right = right_ref[c, k]
                for d in range(2):
                    term = left(c, d, k)[None] * right
                    acc[c][d] = term if acc[c][d] is None else acc[c][d] + term
        return acc

    def pair(p, carry):
        m = product(lambda c, d, k: gd_ref[c, 2 * p + d, k], sn_ref, [[None, None] for _ in range(3)])
        upper = iota((groups, 8, energies), 1) < atoms
        for d in range(2):
            lr = m[0][d] - m[1][d]
            li = m[2][d] - (m[0][d] + m[1][d])
            for c, x in enumerate((lr, li, lr + li)):
                turned = pltpu.roll(x, atoms, 1)
                first = jnp.where(upper, x, turned)
                second = jnp.where(upper, turned, x)
                ld_ref[c, d] = jnp.stack([first, second], axis=1).reshape(orb, 8, energies)
        m = product(lambda c, d, k: ld_ref[c, d, k], gn_ref, [[None, None] for _ in range(3)])
        for d in range(2):
            i = 2 * p + d
            ur = gn_ref[0, i] + (m[0][d] - m[1][d])
            ui = gn_ref[1, i] + (m[2][d] - (m[0][d] + m[1][d]))
            out_ref[0, i] = ur.reshape(orb * atoms, energies).astype(BF16)
            out_ref[1, i] = ui.reshape(orb * atoms, energies).astype(BF16)
        return carry

    lax.fori_loop(0, orb // 2, pair, 0)


def move(value, axis, target):
    count = lax.axis_size(axis)
    return lax.ppermute(value, axis, [(i, target(i) % count) for i in range(count)])


def ring(value, axis, step):
    return move(value, axis, lambda i: i + step)


def pair(i):
    return i ^ 1


def relay(i, count):
    if i & 1:
        return i - 2 if i > 1 else 0
    return i + 2 if i + 2 < count else count - 1


def move_far(value):
    atoms, energies = lax.axis_size("atom"), lax.axis_size("energy")
    moves = []
    for a in range(atoms):
        b = a + 1 if a & 1 else a - 1
        for e in range(energies):
            target = (b, e) if 0 <= b < atoms else (a, (e ^ 1) % energies)
            moves.append((a * energies + e, target[0] * energies + target[1]))
    return lax.ppermute(value, ("atom", "energy"), moves)


def per_device(bare_green, coupling_grad, neighbours, shifts, strength, occupation):
    _, orb, _, atoms, energies = bare_green.shape
    bonds = coupling_grad.shape[0]
    rows = orb * orb * atoms
    span = orb * atoms
    cols = -(-rows // LANES) * LANES
    period = span * LANES // math.gcd(span, LANES)
    early = orb // 3
    late = 2 * (orb - early) * span + 2 * span
    vmem = pl.BlockSpec(memory_space=pltpu.VMEM)
    smem = pl.BlockSpec(memory_space=pltpu.SMEM)
    small = pltpu.CompilerParams(vmem_limit_bytes=20 * 1024 * 1024)

    def shape(*dims, kind=BF16):
        return jax.ShapeDtypeStruct(dims, kind)

    def call(kernel, name, out_shape, *operands, scratch=(), scalars=()):
        return pl.pallas_call(
            kernel, out_shape=out_shape, name=name,
            in_specs=[smem if i in scalars else vmem for i in range(len(operands))],
            out_specs=jax.tree.map(lambda _: vmem, out_shape),
            scratch_shapes=scratch, compiler_params=small,
        )(*operands)

    green = bare_green.reshape(2, rows, energies)
    near = move(green, "atom", pair)
    grads = jnp.transpose(coupling_grad, (0, 1, 3, 2)).reshape(bonds * orb * atoms, orb)
    phonons = [x[None] for x in (shifts, strength, occupation)]
    fetched = [pltpu.with_memory_space_constraint(x, pltpu.HBM) for x in (green, grads, neighbours, *phonons)]
    edge, held, grads, near_atoms, *phonons = pl.pallas_call(
        functools.partial(pack_kernel, orb), name="pack",
        out_shape=[shape(2 * span, LANES), shape(2, rows, energies), shape(*grads.shape),
                   shape(bonds, 16, LANES, kind=jnp.int32)] + [shape(*x.shape, kind=x.dtype) for x in phonons],
        in_specs=[pl.BlockSpec(memory_space=pltpu.HBM)] * 6, out_specs=[vmem] * 7,
        scratch_shapes=[pltpu.SMEM(neighbours.shape, jnp.int32), pltpu.SemaphoreType.DMA((6,))],
        compiler_params=small,
    )(*fetched)
    left, right, table = call(
        functools.partial(factors_kernel, orb, atoms), "factors",
        [shape(bonds, orb, 16, cols), shape(3, bonds, span // 16, 16, period), shape(orb, energies + LANES, energies)],
        grads, near_atoms, *phonons)
    join, rim = call(
        join_kernel, "join", [shape(late, energies), shape(2 * span, LANES)],
        ring(edge, "energy", 1), ring(edge, "energy", -1), held, table)
    far_join = move_far(join)
    rim_near = move(rim, "atom", pair)
    passed = call(pass_kernel, "pass", shape(2, early * span, energies), near, join)
    far_first = move(passed, "atom", lambda i: relay(i, lax.axis_size("atom")))
    weight = shape(orb, span, cols)
    plain = shape(3, orb, span // 8, 8, energies, kind=F32)
    w_near, w_own, w_far, own, gn, gd = call(
        functools.partial(weights_kernel, orb, atoms), "weights",
        [weight, weight, weight, shape(rows, 2 * energies, kind=F32),
         plain, shape(3, orb, orb, 8, energies, kind=F32)],
        left, right, table, held, rim)

    result = call(
        functools.partial(final_kernel, orb, atoms), "green_update", shape(2, orb, span, energies),
        near, rim_near, far_first, far_join, w_near, w_far, own, table, gn, gd,
        scratch=[pltpu.VMEM(plain.shape, F32), pltpu.VMEM((3, 2, orb, 8, energies), F32)])
    return result.reshape(bare_green.shape)


def solution(mesh):
    placed = (
        P(None, None, None, "atom", "energy"),
        P(None, None, None, "atom"),
        P("atom", None),
        P(),
        P(),
        P(),
    )
    return jax.shard_map(
        per_device,
        mesh=mesh,
        in_specs=placed,
        out_specs=P(None, None, None, "atom", "energy"),
        check_vma=False,
    )
```

```python
import functools
import math
import jax
import jax.numpy as jnp
from jax import lax
from jax.experimental import pallas as pl
from jax.experimental.pallas import tpu as pltpu
from jax.sharding import PartitionSpec as P

WIDTH = 4
EDGE = 2 * WIDTH
LANES = 128
F32 = jnp.float32
BF16 = jnp.bfloat16


def iota(shape, axis):
    return lax.broadcasted_iota(jnp.int32, shape, axis)


def dot(a, b, dims=((1,), (0,))):
    return lax.dot_general(a, b, (dims, ((), ())), preferred_element_type=F32)


def steps_below(x, step, most):
    return sum((x >= step * m).astype(jnp.int32) for m in range(1, most))


def pack_kernel(orb, g_hbm, c_hbm, nbr_hbm, sh_hbm, st_hbm, oc_hbm,
                edge_ref, g_ref, c_ref, near_ref, sh_ref, st_ref, oc_ref, nbr_ref, sems):
    ends = ((g_hbm, g_ref), (nbr_hbm, nbr_ref), (c_hbm, c_ref), (sh_hbm, sh_ref), (st_hbm, st_ref), (oc_hbm, oc_ref))
    copies = [pltpu.make_async_copy(source, target, sems.at[i]) for i, (source, target) in enumerate(ends)]
    for copy in copies:
        copy.start()
    copies[0].wait()
    span = g_ref.shape[1] // orb
    lane = iota((span, LANES), 1)
    for r in range(2):
        total = jnp.zeros((span, LANES), F32)
        for k in range(orb):
            x = g_ref[r, k * span:(k + 1) * span].astype(F32)
            turned = pltpu.roll(x, EDGE * k + WIDTH, 1)
            total = jnp.where((lane >= EDGE * k) & (lane < EDGE * (k + 1)), turned, total)
        edge_ref[r * span:(r + 1) * span] = total.astype(BF16)
    copies[1].wait()
    atoms, bonds = nbr_ref.shape
    own = iota(near_ref.shape[1:], 0) & (atoms - 1)
    for n in range(bonds):
        near = jnp.zeros(near_ref.shape[1:], jnp.int32)
        for a in range(atoms):
            near = jnp.where(own == a, nbr_ref[a, n], near)
        near_ref[n] = near
    for copy in copies[2:]:
        copy.wait()


def join_kernel(low_ref, high_ref, g_ref, after_ref, out_ref, rim_ref):
    rows = g_ref.shape[1]
    rim = low_ref.shape[0]
    rest = (out_ref.shape[0] - rim) // 2
    for r in range(2):
        out_ref[r * rest:(r + 1) * rest] = g_ref[r, rows - rest:]
    below = (iota(low_ref.shape, 1) & WIDTH) == 0
    low, high = low_ref[...].astype(F32), high_ref[...].astype(F32)
    halo = jnp.where(below, low, high).astype(BF16)
    out_ref[2 * rest:] = halo
    rim_ref[...] = halo


def pass_kernel(x_ref, after_ref, out_ref):
    out_ref[...] = x_ref[:, :out_ref.shape[1]]


def band_weights(sh_ref, st_ref, oc_ref):
    shifts = sh_ref[...]
    emit = st_ref[...] * oc_ref[...]
    absorb = st_ref[...] * (oc_ref[...] + 1.0)
    zero = jnp.zeros_like(emit)
    weights = []
    for o in range(-WIDTH, WIDTH + 1):
        both = jnp.where(shifts == -o, emit, zero) + jnp.where(shifts == o, absorb, zero)
        weights.append(jnp.sum(both, axis=1, keepdims=True))
    return weights


def banded(weights, gap, keep=None):
    table = jnp.zeros(gap.shape, F32)
    for o in range(-WIDTH, WIDTH + 1):
        hit = gap == o
        if keep is not None:
            hit = hit & keep
        table = jnp.where(hit, weights[o + WIDTH], table)
    return table.astype(BF16)


def factors_kernel(orb, atoms, c_ref, near_ref, sh_ref, st_ref, oc_ref, t1_ref, t2_ref, table_ref):
    bonds = near_ref.shape[0]
    energies = table_ref.shape[2]
    span = orb * atoms
    cols = t1_ref.shape[3]
    period = t2_ref.shape[4]
    here = lax.axis_index("atom")
    place = lax.axis_index("energy")
    last = lax.axis_size("energy") - 1

    weights = band_weights(sh_ref, st_ref, oc_ref)
    band = banded(weights, iota((energies, energies), 0) - iota((energies, energies), 1))
    rim = (LANES, energies)
    row = iota(rim, 0)
    spot = row & (EDGE - 1)
    below = spot < WIDTH
    keep = jnp.where(below, jnp.where(place > 0, 1, 0), jnp.where(place < last, 1, 0)) > 0
    edge = banded(weights, jnp.where(below, spot - WIDTH, spot - WIDTH + energies) - iota(rim, 1), keep)
    for k in range(orb):
        table_ref[k, :energies] = band
        table_ref[k, energies:] = jnp.where((row >= EDGE * k) & (row < EDGE * (k + 1)), edge, jnp.zeros_like(edge))

    c = c_ref[...]
    krow, klane = iota((orb, cols), 0), iota((orb, cols), 1)
    spread = ((klane >= krow * span) & (klane < (krow + 1) * span)).astype(F32).astype(BF16)
    left = dot(c, spread).reshape(bonds * orb * atoms // 8, 8, cols)
    turned = pltpu.roll(left, atoms, 1)
    upper = iota(left.shape, 1) < atoms
    first = jnp.where(upper, left, turned)
    second = jnp.where(upper, turned, left)
    both = jnp.stack([first, second], axis=1).reshape(bonds, orb, 8, cols)
    t1_ref[...] = jnp.concatenate([both, both], axis=2).astype(BF16)

    lrow, llane = iota((orb, period), 0), iota((orb, period), 1)
    inner = llane - span * steps_below(llane, span, period // span)
    spread = ((inner >= lrow * atoms) & (inner < (lrow + 1) * atoms)).astype(F32).astype(BF16)
    right = dot(c, spread).reshape(bonds, span // 16, 16, period)
    odd = here & 1
    base = (here + 1 - 2 * odd, here, here - 1 + 2 * odd)
    other = iota((16, period), 1) & (atoms - 1)
    for n in range(bonds):
        near = jnp.concatenate([near_ref[n]] * (period // LANES), axis=1)
        for s in range(3):
            mask = near == other + base[s] * atoms
            t2_ref[s, n] = jnp.where(mask[None], right[n], 0.0).astype(BF16)


def weights_kernel(orb, atoms, t1_ref, t2_ref, g_ref, wn_ref, wo_ref, gn_ref, gd_ref):
    gr = g_ref[0].astype(F32)
    gi = g_ref[1].astype(F32)
    for c, x in enumerate((gr, gi, gr + gi)):
        gn_ref[c] = x.reshape(gn_ref.shape[1:])
        gd_ref[c] = doubled(x, orb, atoms)
    fill(t1_ref, t2_ref, (wn_ref, wo_ref), 0)


def others_kernel(orb, t1_ref, t2_ref, table_ref, g_ref, rim_ref, wo_ref, wf_ref, s_ref):
    fill(t1_ref, t2_ref, (wf_ref,), 2)
    s_ref[...] = slab_products([wo_ref], [whole(g_ref, orb)], [rim_ref[...]], table_ref)


def fill(t1_ref, t2_ref, outs, first):
    bonds, orb = t1_ref.shape[:2]
    groups, period = t2_ref.shape[2], t2_ref.shape[4]
    for t in range(t1_ref.shape[3] // LANES):
        at = slice(t * LANES, (t + 1) * LANES)
        start = (t * LANES) % period
        cut = slice(start, start + LANES)
        for s, out in enumerate(outs):
            held = [[t2_ref[s + first, n, q, :, cut] for n in range(bonds)] for q in range(groups)]

            def body(i, carry):
                x = [t1_ref[n, i, :, at] for n in range(bonds)]
                for q in range(groups):
                    total = x[0] * held[q][0]
                    for n in range(1, bonds):
                        total = total + x[n] * held[q][n]
                    out[i, q * 16:(q + 1) * 16, at] = total
                return carry

            lax.fori_loop(0, orb, body, 0, unroll=orb)


def rim_of(join_ref, span):
    return join_ref[join_ref.shape[0] - 2 * span:]


def whole(ref, orb):
    return [[(ref.at[0], k), (ref.at[1], k)] for k in range(orb)]


def joined(parts, join_ref, orb, span):
    blocks = []
    for ref in parts:
        blocks += [[(ref.at[0], k), (ref.at[1], k)] for k in range(ref.shape[1] // span)]
    late = orb - len(blocks)
    return blocks + [[(join_ref, k), (join_ref, late + k)] for k in range(late)]


def slab_products(w_refs, slabs, rims, table_ref):
    orb = len(slabs[0])
    span = rims[0].shape[0] // 2
    rims = jnp.concatenate(rims, axis=0)
    summed = []
    for k in range(orb):
        body = jnp.concatenate([ref[i * span:(i + 1) * span] for slab in slabs for ref, i in slab[k]], axis=0)
        summed.append(dot(jnp.concatenate([body, rims], axis=1), table_ref[k]).astype(BF16))
    total = None
    for s, w_ref in enumerate(w_refs):
        at = 2 * s * span
        right = jnp.concatenate(
            [jnp.concatenate([x[at:at + span], x[at + span:at + 2 * span]], axis=1) for x in summed], axis=0)
        rows = right.shape[0]
        w = w_ref[...].reshape(rows, w_ref.shape[2])[:, :rows]
        part = dot(w, right)
        total = part if total is None else total + part
    return total


def doubled(x, orb, atoms):
    pairs = x.reshape(orb * orb * atoms // 8, 8, x.shape[1])
    turned = pltpu.roll(pairs, atoms, 1)
    upper = iota(pairs.shape, 1) < atoms
    first = jnp.where(upper, pairs, turned)
    second = jnp.where(upper, turned, pairs)
    return jnp.stack([first, second], axis=1).reshape(orb, orb, 8, x.shape[1])


def final_kernel(orb, atoms, near_ref, rim_ref, ff_ref, fj_ref, wn_ref, wf_ref, s_ref, table_ref, gn_ref, gd_ref,
                 out_hbm, sn_ref, ld_ref, out_ref, sems):
    energies = table_ref.shape[2]
    span = orb * atoms
    groups = span // 8
    slabs = [whole(near_ref, orb), joined((ff_ref,), fj_ref, orb, span)]
    rims = [rim_ref[...], rim_of(fj_ref, span)]
    total = s_ref[...] + slab_products([wn_ref, wf_ref], slabs, rims, table_ref)
    re, im = total[:, :energies], total[:, energies:]
    for c, x in enumerate((re, im, re + im)):
        sn_ref[c] = x.reshape(orb, groups, 8, energies)

    def product(left, right_ref, acc):
        for k in range(orb):
            for c in range(3):
                right = right_ref[c, k]
                for d in range(2):
                    term = left(c, d, k)[None] * right
                    acc[c][d] = term if acc[c][d] is None else acc[c][d] + term
        return acc

    def sent(p):
        at = pl.ds(2 * p, 2)
        return pltpu.make_async_copy(out_ref.at[:, at], out_hbm.at[:, at], sems.at[p])

    def pair(p, carry):
        m = product(lambda c, d, k: gd_ref[c, 2 * p + d, k], sn_ref, [[None, None] for _ in range(3)])
        upper = iota((groups, 8, energies), 1) < atoms
        for d in range(2):
            lr = m[0][d] - m[1][d]
            li = m[2][d] - (m[0][d] + m[1][d])
            for c, x in enumerate((lr, li, lr + li)):
                turned = pltpu.roll(x, atoms, 1)
                first = jnp.where(upper, x, turned)
                second = jnp.where(upper, turned, x)
                ld_ref[c, d] = jnp.stack([first, second], axis=1).reshape(orb, 8, energies)
        m = product(lambda c, d, k: ld_ref[c, d, k], gn_ref, [[None, None] for _ in range(3)])
        for d in range(2):
            i = 2 * p + d
            ur = gn_ref[0, i] + (m[0][d] - m[1][d])
            ui = gn_ref[1, i] + (m[2][d] - (m[0][d] + m[1][d]))
            out_ref[0, i] = ur.reshape(orb * atoms, energies).astype(BF16)
            out_ref[1, i] = ui.reshape(orb * atoms, energies).astype(BF16)
        sent(p).start()
        return carry

    lax.fori_loop(0, orb // 2, pair, 0, unroll=1)
    for p in range(orb // 2):
        sent(p).wait()


def move(value, axis, target):
    count = lax.axis_size(axis)
    return lax.ppermute(value, axis, [(i, target(i) % count) for i in range(count)])


def ring(value, axis, step):
    return move(value, axis, lambda i: i + step)


def pair(i):
    return i ^ 1


def relay(i, count):
    if i & 1:
        return i - 2 if i > 1 else 0
    return i + 2 if i + 2 < count else count - 1


def move_far(value):
    atoms, energies = lax.axis_size("atom"), lax.axis_size("energy")
    moves = []
    for a in range(atoms):
        b = a + 1 if a & 1 else a - 1
        for e in range(energies):
            target = (b, e) if 0 <= b < atoms else (a, (e ^ 1) % energies)
            moves.append((a * energies + e, target[0] * energies + target[1]))
    return lax.ppermute(value, ("atom", "energy"), moves)


def per_device(bare_green, coupling_grad, neighbours, shifts, strength, occupation):
    _, orb, _, atoms, energies = bare_green.shape
    bonds = coupling_grad.shape[0]
    rows = orb * orb * atoms
    span = orb * atoms
    cols = -(-rows // LANES) * LANES
    period = span * LANES // math.gcd(span, LANES)
    early = orb // 3
    late = 2 * (orb - early) * span + 2 * span
    vmem = pl.BlockSpec(memory_space=pltpu.VMEM)
    smem = pl.BlockSpec(memory_space=pltpu.SMEM)
    small = pltpu.CompilerParams(vmem_limit_bytes=20 * 1024 * 1024)

    def shape(*dims, kind=BF16):
        return jax.ShapeDtypeStruct(dims, kind)

    def call(kernel, name, out_shape, *operands, scratch=(), scalars=()):
        return pl.pallas_call(
            kernel, out_shape=out_shape, name=name,
            in_specs=[smem if i in scalars else vmem for i in range(len(operands))],
            out_specs=jax.tree.map(lambda _: vmem, out_shape),
            scratch_shapes=scratch, compiler_params=small,
        )(*operands)

    green = bare_green.reshape(2, rows, energies)
    near = move(green, "atom", pair)
    grads = jnp.transpose(coupling_grad, (0, 1, 3, 2)).reshape(bonds * orb * atoms, orb)
    phonons = [x[None] for x in (shifts, strength, occupation)]
    fetched = [pltpu.with_memory_space_constraint(x, pltpu.HBM) for x in (green, grads, neighbours, *phonons)]
    edge, held, grads, near_atoms, *phonons = pl.pallas_call(
        functools.partial(pack_kernel, orb), name="pack",
        out_shape=[shape(2 * span, LANES), shape(2, rows, energies), shape(*grads.shape),
                   shape(bonds, 16, LANES, kind=jnp.int32)] + [shape(*x.shape, kind=x.dtype) for x in phonons],
        in_specs=[pl.BlockSpec(memory_space=pltpu.HBM)] * 6, out_specs=[vmem] * 7,
        scratch_shapes=[pltpu.SMEM(neighbours.shape, jnp.int32), pltpu.SemaphoreType.DMA((6,))],
        compiler_params=small,
    )(*fetched)
    left, right, table = call(
        functools.partial(factors_kernel, orb, atoms), "factors",
        [shape(bonds, orb, 16, cols), shape(3, bonds, span // 16, 16, period),
         shape(orb, energies + LANES, energies)],
        grads, near_atoms, *phonons)
    weight = shape(orb, span, cols)
    plain = shape(3, orb, span // 8, 8, energies, kind=F32)
    w_near, w_own, gn, gd = call(
        functools.partial(weights_kernel, orb, atoms), "weights",
        [weight, weight, plain, shape(3, orb, orb, 8, energies, kind=F32)], left, right, held)
    join, rim = call(
        join_kernel, "join", [shape(late, energies), shape(2 * span, LANES)],
        ring(edge, "energy", 1), ring(edge, "energy", -1), held, table)
    far_join = move_far(join)
    rim_near = move(rim, "atom", pair)
    passed = call(pass_kernel, "pass", shape(2, early * span, energies), near, join)
    far_first = move(passed, "atom", lambda i: relay(i, lax.axis_size("atom")))
    w_far, own = call(
        functools.partial(others_kernel, orb), "others", [weight, shape(rows, 2 * energies, kind=F32)],
        left, right, table, held, rim, w_own)

    result = pl.pallas_call(
        functools.partial(final_kernel, orb, atoms), name="green_update",
        out_shape=shape(2, orb, span, energies),
        in_specs=[vmem] * 10, out_specs=pl.BlockSpec(memory_space=pltpu.HBM),
        scratch_shapes=[
            pltpu.VMEM(plain.shape, F32), pltpu.VMEM((3, 2, orb, 8, energies), F32),
            pltpu.VMEM((2, orb, span, energies), BF16), pltpu.SemaphoreType.DMA((orb // 2,))],
        compiler_params=small,
    )(near, rim_near, far_first, far_join, w_near, w_far, own, table, gn, gd)
    return result.reshape(bare_green.shape)


def solution(mesh):
    placed = (
        P(None, None, None, "atom", "energy"),
        P(None, None, None, "atom"),
        P("atom", None),
        P(),
        P(),
        P(),
    )
    return jax.shard_map(
        per_device,
        mesh=mesh,
        in_specs=placed,
        out_specs=P(None, None, None, "atom", "energy"),
        check_vma=False,
    )
```

```python
import functools
import math
import jax
import jax.numpy as jnp
from jax import lax
from jax.experimental import pallas as pl
from jax.experimental.pallas import tpu as pltpu
from jax.sharding import PartitionSpec as P

WIDTH = 4
EDGE = 2 * WIDTH
LANES = 128
F32 = jnp.float32
BF16 = jnp.bfloat16


def iota(shape, axis):
    return lax.broadcasted_iota(jnp.int32, shape, axis)


def dot(a, b, dims=((1,), (0,))):
    return lax.dot_general(a, b, (dims, ((), ())), preferred_element_type=F32)


def steps_below(x, step, most):
    return sum((x >= step * m).astype(jnp.int32) for m in range(1, most))


def pack_kernel(orb, g_hbm, c_hbm, nbr_hbm, sh_hbm, st_hbm, oc_hbm,
                edge_ref, g_ref, c_ref, near_ref, sh_ref, st_ref, oc_ref, nbr_ref, sems):
    ends = ((g_hbm, g_ref), (nbr_hbm, nbr_ref), (c_hbm, c_ref), (sh_hbm, sh_ref), (st_hbm, st_ref), (oc_hbm, oc_ref))
    copies = [pltpu.make_async_copy(source, target, sems.at[i]) for i, (source, target) in enumerate(ends)]
    for copy in copies:
        copy.start()
    copies[0].wait()
    span = g_ref.shape[1] // orb
    lane = iota((span, LANES), 1)
    for r in range(2):
        total = jnp.zeros((span, LANES), F32)
        for k in range(orb):
            x = g_ref[r, k * span:(k + 1) * span].astype(F32)
            turned = pltpu.roll(x, EDGE * k + WIDTH, 1)
            total = jnp.where((lane >= EDGE * k) & (lane < EDGE * (k + 1)), turned, total)
        edge_ref[r * span:(r + 1) * span] = total.astype(BF16)
    copies[1].wait()
    atoms, bonds = nbr_ref.shape
    own = iota(near_ref.shape[1:], 0) & (atoms - 1)
    for n in range(bonds):
        near = jnp.zeros(near_ref.shape[1:], jnp.int32)
        for a in range(atoms):
            near = jnp.where(own == a, nbr_ref[a, n], near)
        near_ref[n] = near
    for copy in copies[2:]:
        copy.wait()


def join_kernel(low_ref, high_ref, g_ref, after_ref, out_ref, rim_ref):
    rows = g_ref.shape[1]
    rim = low_ref.shape[0]
    rest = (out_ref.shape[0] - rim) // 2
    for r in range(2):
        out_ref[r * rest:(r + 1) * rest] = g_ref[r, rows - rest:]
    below = ((iota(low_ref.shape, 1) & WIDTH) == 0) ^ ((lax.axis_index("energy") & 1) == 0)
    low, high = low_ref[...].astype(F32), high_ref[...].astype(F32)
    halo = jnp.where(below, low, high).astype(BF16)
    out_ref[2 * rest:] = halo
    rim_ref[...] = halo


def pass_kernel(x_ref, after_ref, out_ref):
    out_ref[...] = x_ref[:, :out_ref.shape[1]]


def band_weights(sh_ref, st_ref, oc_ref):
    shifts = sh_ref[...]
    emit = st_ref[...] * oc_ref[...]
    absorb = st_ref[...] * (oc_ref[...] + 1.0)
    zero = jnp.zeros_like(emit)
    weights = []
    for o in range(-WIDTH, WIDTH + 1):
        both = jnp.where(shifts == -o, emit, zero) + jnp.where(shifts == o, absorb, zero)
        weights.append(jnp.sum(both, axis=1, keepdims=True))
    return weights


def banded(weights, gap, keep=None):
    table = jnp.zeros(gap.shape, F32)
    for o in range(-WIDTH, WIDTH + 1):
        hit = gap == o
        if keep is not None:
            hit = hit & keep
        table = jnp.where(hit, weights[o + WIDTH], table)
    return table.astype(BF16)


def factors_kernel(orb, atoms, c_ref, near_ref, sh_ref, st_ref, oc_ref, t1_ref, t2_ref, table_ref):
    bonds = near_ref.shape[0]
    energies = table_ref.shape[2]
    span = orb * atoms
    cols = t1_ref.shape[3]
    period = t2_ref.shape[4]
    here = lax.axis_index("atom")
    place = lax.axis_index("energy")
    last = lax.axis_size("energy") - 1

    weights = band_weights(sh_ref, st_ref, oc_ref)
    band = banded(weights, iota((energies, energies), 0) - iota((energies, energies), 1))
    rim = (LANES, energies)
    row = iota(rim, 0)
    spot = row & (EDGE - 1)
    below = spot < WIDTH
    keep = jnp.where(below, jnp.where(place > 0, 1, 0), jnp.where(place < last, 1, 0)) > 0
    edge = banded(weights, jnp.where(below, spot - WIDTH, spot - WIDTH + energies) - iota(rim, 1), keep)
    for k in range(orb):
        table_ref[k, :energies] = band
        table_ref[k, energies:] = jnp.where((row >= EDGE * k) & (row < EDGE * (k + 1)), edge, jnp.zeros_like(edge))

    c = c_ref[...]
    krow, klane = iota((orb, cols), 0), iota((orb, cols), 1)
    spread = ((klane >= krow * span) & (klane < (krow + 1) * span)).astype(F32).astype(BF16)
    left = dot(c, spread).reshape(bonds * orb * atoms // 8, 8, cols)
    turned = pltpu.roll(left, atoms, 1)
    upper = iota(left.shape, 1) < atoms
    first = jnp.where(upper, left, turned)
    second = jnp.where(upper, turned, left)
    both = jnp.stack([first, second], axis=1).reshape(bonds, orb, 8, cols)
    t1_ref[...] = jnp.concatenate([both, both], axis=2).astype(BF16)

    lrow, llane = iota((orb, period), 0), iota((orb, period), 1)
    inner = llane - span * steps_below(llane, span, period // span)
    spread = ((inner >= lrow * atoms) & (inner < (lrow + 1) * atoms)).astype(F32).astype(BF16)
    right = dot(c, spread).reshape(bonds, span // 16, 16, period)
    odd = here & 1
    base = (here + 1 - 2 * odd, here, here - 1 + 2 * odd)
    other = iota((16, period), 1) & (atoms - 1)
    for n in range(bonds):
        near = jnp.concatenate([near_ref[n]] * (period // LANES), axis=1)
        for s in range(3):
            mask = near == other + base[s] * atoms
            t2_ref[s, n] = jnp.where(mask[None], right[n], 0.0).astype(BF16)


def weights_kernel(orb, atoms, t1_ref, t2_ref, g_ref, wn_ref, wo_ref, gn_ref, gd_ref):
    gr = g_ref[0].astype(F32)
    gi = g_ref[1].astype(F32)
    for c, x in enumerate((gr, gi, gr + gi)):
        gn_ref[c] = x.reshape(gn_ref.shape[1:])
        gd_ref[c] = doubled(x, orb, atoms)
    fill(t1_ref, t2_ref, (wn_ref, wo_ref), 0)


def others_kernel(orb, t1_ref, t2_ref, table_ref, g_ref, rim_ref, wo_ref, wf_ref, s_ref):
    fill(t1_ref, t2_ref, (wf_ref,), 2)
    s_ref[...] = slab_products([wo_ref], [whole(g_ref, orb)], [rim_ref[...]], table_ref)


def fill(t1_ref, t2_ref, outs, first):
    bonds, orb = t1_ref.shape[:2]
    groups, period = t2_ref.shape[2], t2_ref.shape[4]
    for t in range(t1_ref.shape[3] // LANES):
        at = slice(t * LANES, (t + 1) * LANES)
        start = (t * LANES) % period
        cut = slice(start, start + LANES)
        for s, out in enumerate(outs):
            held = [[t2_ref[s + first, n, q, :, cut] for n in range(bonds)] for q in range(groups)]

            def body(i, carry):
                x = [t1_ref[n, i, :, at] for n in range(bonds)]
                for q in range(groups):
                    total = x[0] * held[q][0]
                    for n in range(1, bonds):
                        total = total + x[n] * held[q][n]
                    out[i, q * 16:(q + 1) * 16, at] = total
                return carry

            lax.fori_loop(0, orb, body, 0, unroll=orb)


def rim_of(join_ref, span):
    return join_ref[join_ref.shape[0] - 2 * span:]


def whole(ref, orb):
    return [[(ref.at[0], k), (ref.at[1], k)] for k in range(orb)]


def joined(parts, join_ref, orb, span):
    blocks = []
    for ref in parts:
        blocks += [[(ref.at[0], k), (ref.at[1], k)] for k in range(ref.shape[1] // span)]
    late = orb - len(blocks)
    return blocks + [[(join_ref, k), (join_ref, late + k)] for k in range(late)]


def slab_products(w_refs, slabs, rims, table_ref):
    orb = len(slabs[0])
    span = rims[0].shape[0] // 2
    rims = jnp.concatenate(rims, axis=0)
    summed = []
    for k in range(orb):
        body = jnp.concatenate([ref[i * span:(i + 1) * span] for slab in slabs for ref, i in slab[k]], axis=0)
        summed.append(dot(jnp.concatenate([body, rims], axis=1), table_ref[k]).astype(BF16))
    total = None
    for s, w_ref in enumerate(w_refs):
        at = 2 * s * span
        right = jnp.concatenate(
            [jnp.concatenate([x[at:at + span], x[at + span:at + 2 * span]], axis=1) for x in summed], axis=0)
        rows = right.shape[0]
        w = w_ref[...].reshape(rows, w_ref.shape[2])[:, :rows]
        part = dot(w, right)
        total = part if total is None else total + part
    return total


def doubled(x, orb, atoms):
    pairs = x.reshape(orb * orb * atoms // 8, 8, x.shape[1])
    turned = pltpu.roll(pairs, atoms, 1)
    upper = iota(pairs.shape, 1) < atoms
    first = jnp.where(upper, pairs, turned)
    second = jnp.where(upper, turned, pairs)
    return jnp.stack([first, second], axis=1).reshape(orb, orb, 8, x.shape[1])


def final_kernel(orb, atoms, near_ref, rim_ref, ff_ref, fj_ref, wn_ref, wf_ref, s_ref, table_ref, gn_ref, gd_ref,
                 out_hbm, sn_ref, ld_ref, out_ref, sems):
    energies = table_ref.shape[2]
    span = orb * atoms
    groups = span // 8
    slabs = [whole(near_ref, orb), joined((ff_ref,), fj_ref, orb, span)]
    rims = [rim_ref[...], rim_of(fj_ref, span)]
    total = s_ref[...] + slab_products([wn_ref, wf_ref], slabs, rims, table_ref)
    re, im = total[:, :energies], total[:, energies:]
    for c, x in enumerate((re, im, re + im)):
        sn_ref[c] = x.reshape(orb, groups, 8, energies)

    def product(left, right_ref, acc):
        for k in range(orb):
            for c in range(3):
                right = right_ref[c, k]
                for d in range(2):
                    term = left(c, d, k)[None] * right
                    acc[c][d] = term if acc[c][d] is None else acc[c][d] + term
        return acc

    def sent(p):
        at = pl.ds(2 * p, 2)
        return pltpu.make_async_copy(out_ref.at[:, at], out_hbm.at[:, at], sems.at[p])

    def pair(p, carry):
        m = product(lambda c, d, k: gd_ref[c, 2 * p + d, k], sn_ref, [[None, None] for _ in range(3)])
        upper = iota((groups, 8, energies), 1) < atoms
        for d in range(2):
            lr = m[0][d] - m[1][d]
            li = m[2][d] - (m[0][d] + m[1][d])
            for c, x in enumerate((lr, li, lr + li)):
                turned = pltpu.roll(x, atoms, 1)
                first = jnp.where(upper, x, turned)
                second = jnp.where(upper, turned, x)
                ld_ref[c, d] = jnp.stack([first, second], axis=1).reshape(orb, 8, energies)
        m = product(lambda c, d, k: ld_ref[c, d, k], gn_ref, [[None, None] for _ in range(3)])
        for d in range(2):
            i = 2 * p + d
            ur = gn_ref[0, i] + (m[0][d] - m[1][d])
            ui = gn_ref[1, i] + (m[2][d] - (m[0][d] + m[1][d]))
            out_ref[0, i] = ur.reshape(orb * atoms, energies).astype(BF16)
            out_ref[1, i] = ui.reshape(orb * atoms, energies).astype(BF16)
        sent(p).start()
        return carry

    lax.fori_loop(0, orb // 2, pair, 0, unroll=1)
    for p in range(orb // 2):
        sent(p).wait()


def move(value, axis, target):
    count = lax.axis_size(axis)
    return lax.ppermute(value, axis, [(i, target(i) % count) for i in range(count)])


def ring(value, axis, step):
    return move(value, axis, lambda i: i + step)


def pair(i):
    return i ^ 1


def cross(i):
    return i + 1 if i & 1 else i - 1


def relay(i, count):
    if i & 1:
        return i - 2 if i > 1 else 0
    return i + 2 if i + 2 < count else count - 1


def move_far(value):
    atoms, energies = lax.axis_size("atom"), lax.axis_size("energy")
    moves = []
    for a in range(atoms):
        b = a + 1 if a & 1 else a - 1
        for e in range(energies):
            target = (b, e) if 0 <= b < atoms else (a, (e ^ 1) % energies)
            moves.append((a * energies + e, target[0] * energies + target[1]))
    return lax.ppermute(value, ("atom", "energy"), moves)


def per_device(bare_green, coupling_grad, neighbours, shifts, strength, occupation):
    _, orb, _, atoms, energies = bare_green.shape
    bonds = coupling_grad.shape[0]
    rows = orb * orb * atoms
    span = orb * atoms
    cols = -(-rows // LANES) * LANES
    period = span * LANES // math.gcd(span, LANES)
    early = orb // 2
    late = 2 * (orb - early) * span + 2 * span
    vmem = pl.BlockSpec(memory_space=pltpu.VMEM)
    smem = pl.BlockSpec(memory_space=pltpu.SMEM)
    small = pltpu.CompilerParams(vmem_limit_bytes=20 * 1024 * 1024)

    def shape(*dims, kind=BF16):
        return jax.ShapeDtypeStruct(dims, kind)

    def call(kernel, name, out_shape, *operands, scratch=(), scalars=()):
        return pl.pallas_call(
            kernel, out_shape=out_shape, name=name,
            in_specs=[smem if i in scalars else vmem for i in range(len(operands))],
            out_specs=jax.tree.map(lambda _: vmem, out_shape),
            scratch_shapes=scratch, compiler_params=small,
        )(*operands)

    green = bare_green.reshape(2, rows, energies)
    near = move(green, "atom", pair)
    grads = jnp.transpose(coupling_grad, (0, 1, 3, 2)).reshape(bonds * orb * atoms, orb)
    phonons = [x[None] for x in (shifts, strength, occupation)]
    fetched = [pltpu.with_memory_space_constraint(x, pltpu.HBM) for x in (green, grads, neighbours, *phonons)]
    edge, held, grads, near_atoms, *phonons = pl.pallas_call(
        functools.partial(pack_kernel, orb), name="pack",
        out_shape=[shape(2 * span, LANES), shape(2, rows, energies), shape(*grads.shape),
                   shape(bonds, 16, LANES, kind=jnp.int32)] + [shape(*x.shape, kind=x.dtype) for x in phonons],
        in_specs=[pl.BlockSpec(memory_space=pltpu.HBM)] * 6, out_specs=[vmem] * 7,
        scratch_shapes=[pltpu.SMEM(neighbours.shape, jnp.int32), pltpu.SemaphoreType.DMA((6,))],
        compiler_params=small,
    )(*fetched)
    left, right, table = call(
        functools.partial(factors_kernel, orb, atoms), "factors",
        [shape(bonds, orb, 16, cols), shape(3, bonds, span // 16, 16, period),
         shape(orb, energies + LANES, energies)],
        grads, near_atoms, *phonons)
    weight = shape(orb, span, cols)
    plain = shape(3, orb, span // 8, 8, energies, kind=F32)
    w_near, w_own, gn, gd = call(
        functools.partial(weights_kernel, orb, atoms), "weights",
        [weight, weight, plain, shape(3, orb, orb, 8, energies, kind=F32)], left, right, held)
    join, rim = call(
        join_kernel, "join", [shape(late, energies), shape(2 * span, LANES)],
        move(edge, "energy", pair), move(edge, "energy", cross), held, table)
    far_join = move_far(join)
    rim_near = move(rim, "atom", pair)
    passed = call(pass_kernel, "pass", shape(2, early * span, energies), near, join)
    far_first = move(passed, "atom", lambda i: relay(i, lax.axis_size("atom")))
    w_far, own = call(
        functools.partial(others_kernel, orb), "others", [weight, shape(rows, 2 * energies, kind=F32)],
        left, right, table, held, rim, w_own)

    result = pl.pallas_call(
        functools.partial(final_kernel, orb, atoms), name="green_update",
        out_shape=shape(2, orb, span, energies),
        in_specs=[vmem] * 10, out_specs=pl.BlockSpec(memory_space=pltpu.HBM),
        scratch_shapes=[
            pltpu.VMEM(plain.shape, F32), pltpu.VMEM((3, 2, orb, 8, energies), F32),
            pltpu.VMEM((2, orb, span, energies), BF16), pltpu.SemaphoreType.DMA((orb // 2,))],
        compiler_params=small,
    )(near, rim_near, far_first, far_join, w_near, w_far, own, table, gn, gd)
    return result.reshape(bare_green.shape)


def solution(mesh):
    placed = (
        P(None, None, None, "atom", "energy"),
        P(None, None, None, "atom"),
        P("atom", None),
        P(),
        P(),
        P(),
    )
    return jax.shard_map(
        per_device,
        mesh=mesh,
        in_specs=placed,
        out_specs=P(None, None, None, "atom", "energy"),
        check_vma=False,
    )
```

```python
import functools
import math
import jax
import jax.numpy as jnp
from jax import lax
from jax.experimental import pallas as pl
from jax.experimental.pallas import tpu as pltpu
from jax.sharding import PartitionSpec as P

WIDTH = 4
EDGE = 2 * WIDTH
LANES = 128
F32 = jnp.float32
BF16 = jnp.bfloat16


def iota(shape, axis):
    return lax.broadcasted_iota(jnp.int32, shape, axis)


def dot(a, b, dims=((1,), (0,))):
    return lax.dot_general(a, b, (dims, ((), ())), preferred_element_type=F32)


def steps_below(x, step, most):
    return sum((x >= step * m).astype(jnp.int32) for m in range(1, most))


def pack_edges(orb, g_ref, edge_ref):
    span = g_ref.shape[1] // orb
    lane = iota((span, LANES), 1)
    for r in range(2):
        total = jnp.zeros((span, LANES), F32)
        for k in range(orb):
            x = g_ref[r, k * span:(k + 1) * span].astype(F32)
            turned = pltpu.roll(x, EDGE * k + WIDTH, 1)
            total = jnp.where((lane >= EDGE * k) & (lane < EDGE * (k + 1)), turned, total)
        edge_ref[r * span:(r + 1) * span] = total.astype(BF16)


def from_sides(pair_ref, cross_ref):
    below = ((iota(pair_ref.shape, 1) & WIDTH) == 0) ^ ((lax.axis_index("energy") & 1) == 0)
    return jnp.where(below, pair_ref[...].astype(F32), cross_ref[...].astype(F32)).astype(BF16)


def pack_kernel(orb, g_hbm, c_hbm, nbr_hbm, sh_hbm, st_hbm, oc_hbm,
                edge_ref, g_ref, c_ref, near_ref, sh_ref, st_ref, oc_ref, nbr_ref, sems):
    ends = ((g_hbm, g_ref), (nbr_hbm, nbr_ref), (c_hbm, c_ref), (sh_hbm, sh_ref), (st_hbm, st_ref), (oc_hbm, oc_ref))
    copies = [pltpu.make_async_copy(source, target, sems.at[i]) for i, (source, target) in enumerate(ends)]
    for copy in copies:
        copy.start()
    copies[0].wait()
    pack_edges(orb, g_ref, edge_ref)
    copies[1].wait()
    atoms, bonds = nbr_ref.shape
    own = iota(near_ref.shape[1:], 0) & (atoms - 1)
    for n in range(bonds):
        near = jnp.zeros(near_ref.shape[1:], jnp.int32)
        for a in range(atoms):
            near = jnp.where(own == a, nbr_ref[a, n], near)
        near_ref[n] = near
    for copy in copies[2:]:
        copy.wait()


def join_kernel(pair_ref, cross_ref, g_ref, after_ref, out_ref, rim_ref):
    rows = g_ref.shape[1]
    rim = pair_ref.shape[0]
    rest = (out_ref.shape[0] - rim) // 2
    for r in range(2):
        out_ref[r * rest:(r + 1) * rest] = g_ref[r, rows - rest:]
    halo = from_sides(pair_ref, cross_ref)
    out_ref[2 * rest:] = halo
    rim_ref[...] = halo


def pass_kernel(orb, x_ref, after_ref, out_ref, edge_ref):
    out_ref[...] = x_ref[:, :out_ref.shape[1]]
    pack_edges(orb, x_ref, edge_ref)


def band_weights(sh_ref, st_ref, oc_ref):
    shifts = sh_ref[...]
    emit = st_ref[...] * oc_ref[...]
    absorb = st_ref[...] * (oc_ref[...] + 1.0)
    zero = jnp.zeros_like(emit)
    weights = []
    for o in range(-WIDTH, WIDTH + 1):
        both = jnp.where(shifts == -o, emit, zero) + jnp.where(shifts == o, absorb, zero)
        weights.append(jnp.sum(both, axis=1, keepdims=True))
    return weights


def banded(weights, gap, keep=None):
    table = jnp.zeros(gap.shape, F32)
    for o in range(-WIDTH, WIDTH + 1):
        hit = gap == o
        if keep is not None:
            hit = hit & keep
        table = jnp.where(hit, weights[o + WIDTH], table)
    return table.astype(BF16)


def factors_kernel(orb, atoms, c_ref, near_ref, sh_ref, st_ref, oc_ref, t1_ref, t2_ref, table_ref):
    bonds = near_ref.shape[0]
    energies = table_ref.shape[2]
    span = orb * atoms
    cols = t1_ref.shape[3]
    period = t2_ref.shape[4]
    here = lax.axis_index("atom")
    place = lax.axis_index("energy")
    last = lax.axis_size("energy") - 1

    weights = band_weights(sh_ref, st_ref, oc_ref)
    band = banded(weights, iota((energies, energies), 0) - iota((energies, energies), 1))
    rim = (LANES, energies)
    row = iota(rim, 0)
    spot = row & (EDGE - 1)
    below = spot < WIDTH
    keep = jnp.where(below, jnp.where(place > 0, 1, 0), jnp.where(place < last, 1, 0)) > 0
    edge = banded(weights, jnp.where(below, spot - WIDTH, spot - WIDTH + energies) - iota(rim, 1), keep)
    for k in range(orb):
        table_ref[k, :energies] = band
        table_ref[k, energies:] = jnp.where((row >= EDGE * k) & (row < EDGE * (k + 1)), edge, jnp.zeros_like(edge))

    c = c_ref[...]
    krow, klane = iota((orb, cols), 0), iota((orb, cols), 1)
    spread = ((klane >= krow * span) & (klane < (krow + 1) * span)).astype(F32).astype(BF16)
    left = dot(c, spread).reshape(bonds * orb * atoms // 8, 8, cols)
    turned = pltpu.roll(left, atoms, 1)
    upper = iota(left.shape, 1) < atoms
    first = jnp.where(upper, left, turned)
    second = jnp.where(upper, turned, left)
    both = jnp.stack([first, second], axis=1).reshape(bonds, orb, 8, cols)
    t1_ref[...] = jnp.concatenate([both, both], axis=2).astype(BF16)

    lrow, llane = iota((orb, period), 0), iota((orb, period), 1)
    inner = llane - span * steps_below(llane, span, period // span)
    spread = ((inner >= lrow * atoms) & (inner < (lrow + 1) * atoms)).astype(F32).astype(BF16)
    right = dot(c, spread).reshape(bonds, span // 16, 16, period)
    odd = here & 1
    base = (here + 1 - 2 * odd, here, here - 1 + 2 * odd)
    other = iota((16, period), 1) & (atoms - 1)
    for n in range(bonds):
        near = jnp.concatenate([near_ref[n]] * (period // LANES), axis=1)
        for s in range(3):
            mask = near == other + base[s] * atoms
            t2_ref[s, n] = jnp.where(mask[None], right[n], 0.0).astype(BF16)


def weights_kernel(orb, atoms, t1_ref, t2_ref, g_ref, wn_ref, wo_ref, gn_ref, gd_ref):
    gr = g_ref[0].astype(F32)
    gi = g_ref[1].astype(F32)
    for c, x in enumerate((gr, gi, gr + gi)):
        gn_ref[c] = x.reshape(gn_ref.shape[1:])
        gd_ref[c] = doubled(x, orb, atoms)
    fill(t1_ref, t2_ref, (wn_ref, wo_ref), 0)


def others_kernel(orb, t1_ref, t2_ref, table_ref, g_ref, rim_ref, wo_ref, wf_ref, s_ref):
    fill(t1_ref, t2_ref, (wf_ref,), 2)
    s_ref[...] = slab_products([wo_ref], [whole(g_ref, orb)], [rim_ref[...]], table_ref)


def fill(t1_ref, t2_ref, outs, first):
    bonds, orb = t1_ref.shape[:2]
    groups, period = t2_ref.shape[2], t2_ref.shape[4]
    for t in range(t1_ref.shape[3] // LANES):
        at = slice(t * LANES, (t + 1) * LANES)
        start = (t * LANES) % period
        cut = slice(start, start + LANES)
        for s, out in enumerate(outs):
            held = [[t2_ref[s + first, n, q, :, cut] for n in range(bonds)] for q in range(groups)]

            def body(i, carry):
                x = [t1_ref[n, i, :, at] for n in range(bonds)]
                for q in range(groups):
                    total = x[0] * held[q][0]
                    for n in range(1, bonds):
                        total = total + x[n] * held[q][n]
                    out[i, q * 16:(q + 1) * 16, at] = total
                return carry

            lax.fori_loop(0, orb, body, 0, unroll=orb)


def rim_of(join_ref, span):
    return join_ref[join_ref.shape[0] - 2 * span:]


def whole(ref, orb):
    return [[(ref.at[0], k), (ref.at[1], k)] for k in range(orb)]


def joined(parts, join_ref, orb, span):
    blocks = []
    for ref in parts:
        blocks += [[(ref.at[0], k), (ref.at[1], k)] for k in range(ref.shape[1] // span)]
    late = orb - len(blocks)
    return blocks + [[(join_ref, k), (join_ref, late + k)] for k in range(late)]


def slab_products(w_refs, slabs, rims, table_ref):
    orb = len(slabs[0])
    span = rims[0].shape[0] // 2
    rims = jnp.concatenate(rims, axis=0)
    summed = []
    for k in range(orb):
        body = jnp.concatenate([ref[i * span:(i + 1) * span] for slab in slabs for ref, i in slab[k]], axis=0)
        summed.append(dot(jnp.concatenate([body, rims], axis=1), table_ref[k]).astype(BF16))
    total = None
    for s, w_ref in enumerate(w_refs):
        at = 2 * s * span
        right = jnp.concatenate(
            [jnp.concatenate([x[at:at + span], x[at + span:at + 2 * span]], axis=1) for x in summed], axis=0)
        rows = right.shape[0]
        w = w_ref[...].reshape(rows, w_ref.shape[2])[:, :rows]
        part = dot(w, right)
        total = part if total is None else total + part
    return total


def doubled(x, orb, atoms):
    pairs = x.reshape(orb * orb * atoms // 8, 8, x.shape[1])
    turned = pltpu.roll(pairs, atoms, 1)
    upper = iota(pairs.shape, 1) < atoms
    first = jnp.where(upper, pairs, turned)
    second = jnp.where(upper, turned, pairs)
    return jnp.stack([first, second], axis=1).reshape(orb, orb, 8, x.shape[1])


def final_kernel(orb, atoms, near_ref, pair_ref, cross_ref, ff_ref, fj_ref, wn_ref, wf_ref, s_ref, table_ref, gn_ref, gd_ref,
                 out_hbm, sn_ref, ld_ref, out_ref, sems):
    energies = table_ref.shape[2]
    span = orb * atoms
    groups = span // 8
    slabs = [whole(near_ref, orb), joined((ff_ref,), fj_ref, orb, span)]
    rims = [from_sides(pair_ref, cross_ref), rim_of(fj_ref, span)]
    total = s_ref[...] + slab_products([wn_ref, wf_ref], slabs, rims, table_ref)
    re, im = total[:, :energies], total[:, energies:]
    for c, x in enumerate((re, im, re + im)):
        sn_ref[c] = x.reshape(orb, groups, 8, energies)

    def product(left, right_ref, acc):
        for k in range(orb):
            for c in range(3):
                right = right_ref[c, k]
                for d in range(2):
                    term = left(c, d, k)[None] * right
                    acc[c][d] = term if acc[c][d] is None else acc[c][d] + term
        return acc

    def sent(p):
        at = pl.ds(2 * p, 2)
        return pltpu.make_async_copy(out_ref.at[:, at], out_hbm.at[:, at], sems.at[p])

    def pair(p, carry):
        m = product(lambda c, d, k: gd_ref[c, 2 * p + d, k], sn_ref, [[None, None] for _ in range(3)])
        upper = iota((groups, 8, energies), 1) < atoms
        for d in range(2):
            lr = m[0][d] - m[1][d]
            li = m[2][d] - (m[0][d] + m[1][d])
            for c, x in enumerate((lr, li, lr + li)):
                turned = pltpu.roll(x, atoms, 1)
                first = jnp.where(upper, x, turned)
                second = jnp.where(upper, turned, x)
                ld_ref[c, d] = jnp.stack([first, second], axis=1).reshape(orb, 8, energies)
        m = product(lambda c, d, k: ld_ref[c, d, k], gn_ref, [[None, None] for _ in range(3)])
        for d in range(2):
            i = 2 * p + d
            ur = gn_ref[0, i] + (m[0][d] - m[1][d])
            ui = gn_ref[1, i] + (m[2][d] - (m[0][d] + m[1][d]))
            out_ref[0, i] = ur.reshape(orb * atoms, energies).astype(BF16)
            out_ref[1, i] = ui.reshape(orb * atoms, energies).astype(BF16)
        sent(p).start()
        return carry

    lax.fori_loop(0, orb // 2, pair, 0, unroll=1)
    for p in range(orb // 2):
        sent(p).wait()


def move(value, axis, target):
    count = lax.axis_size(axis)
    return lax.ppermute(value, axis, [(i, target(i) % count) for i in range(count)])


def ring(value, axis, step):
    return move(value, axis, lambda i: i + step)


def pair(i):
    return i ^ 1


def cross(i):
    return i + 1 if i & 1 else i - 1


def relay(i, count):
    if i & 1:
        return i - 2 if i > 1 else 0
    return i + 2 if i + 2 < count else count - 1


def move_far(value):
    atoms, energies = lax.axis_size("atom"), lax.axis_size("energy")
    moves = []
    for a in range(atoms):
        b = a + 1 if a & 1 else a - 1
        for e in range(energies):
            target = (b, e) if 0 <= b < atoms else (a, (e ^ 1) % energies)
            moves.append((a * energies + e, target[0] * energies + target[1]))
    return lax.ppermute(value, ("atom", "energy"), moves)


def per_device(bare_green, coupling_grad, neighbours, shifts, strength, occupation):
    _, orb, _, atoms, energies = bare_green.shape
    bonds = coupling_grad.shape[0]
    rows = orb * orb * atoms
    span = orb * atoms
    cols = -(-rows // LANES) * LANES
    period = span * LANES // math.gcd(span, LANES)
    early = orb // 2
    late = 2 * (orb - early) * span + 2 * span
    vmem = pl.BlockSpec(memory_space=pltpu.VMEM)
    smem = pl.BlockSpec(memory_space=pltpu.SMEM)
    small = pltpu.CompilerParams(vmem_limit_bytes=20 * 1024 * 1024)

    def shape(*dims, kind=BF16):
        return jax.ShapeDtypeStruct(dims, kind)

    def call(kernel, name, out_shape, *operands, scratch=(), scalars=()):
        return pl.pallas_call(
            kernel, out_shape=out_shape, name=name,
            in_specs=[smem if i in scalars else vmem for i in range(len(operands))],
            out_specs=jax.tree.map(lambda _: vmem, out_shape),
            scratch_shapes=scratch, compiler_params=small,
        )(*operands)

    green = bare_green.reshape(2, rows, energies)
    near = move(green, "atom", pair)
    grads = jnp.transpose(coupling_grad, (0, 1, 3, 2)).reshape(bonds * orb * atoms, orb)
    phonons = [x[None] for x in (shifts, strength, occupation)]
    fetched = [pltpu.with_memory_space_constraint(x, pltpu.HBM) for x in (green, grads, neighbours, *phonons)]
    edge, held, grads, near_atoms, *phonons = pl.pallas_call(
        functools.partial(pack_kernel, orb), name="pack",
        out_shape=[shape(2 * span, LANES), shape(2, rows, energies), shape(*grads.shape),
                   shape(bonds, 16, LANES, kind=jnp.int32)] + [shape(*x.shape, kind=x.dtype) for x in phonons],
        in_specs=[pl.BlockSpec(memory_space=pltpu.HBM)] * 6, out_specs=[vmem] * 7,
        scratch_shapes=[pltpu.SMEM(neighbours.shape, jnp.int32), pltpu.SemaphoreType.DMA((6,))],
        compiler_params=small,
    )(*fetched)
    left, right, table = call(
        functools.partial(factors_kernel, orb, atoms), "factors",
        [shape(bonds, orb, 16, cols), shape(3, bonds, span // 16, 16, period),
         shape(orb, energies + LANES, energies)],
        grads, near_atoms, *phonons)
    weight = shape(orb, span, cols)
    plain = shape(3, orb, span // 8, 8, energies, kind=F32)
    w_near, w_own, gn, gd = call(
        functools.partial(weights_kernel, orb, atoms), "weights",
        [weight, weight, plain, shape(3, orb, orb, 8, energies, kind=F32)], left, right, held)
    join, rim = call(
        join_kernel, "join", [shape(late, energies), shape(2 * span, LANES)],
        move(edge, "energy", pair), move(edge, "energy", cross), held, w_near)
    far_join = move_far(join)
    passed, near_edge = call(
        functools.partial(pass_kernel, orb), "pack_near",
        [shape(2, early * span, energies), shape(2 * span, LANES)], near, join)
    far_first = move(passed, "atom", lambda i: relay(i, lax.axis_size("atom")))
    w_far, own = call(
        functools.partial(others_kernel, orb), "others", [weight, shape(rows, 2 * energies, kind=F32)],
        left, right, table, held, rim, w_own)

    result = pl.pallas_call(
        functools.partial(final_kernel, orb, atoms), name="green_update",
        out_shape=shape(2, orb, span, energies),
        in_specs=[vmem] * 11, out_specs=pl.BlockSpec(memory_space=pltpu.HBM),
        scratch_shapes=[
            pltpu.VMEM(plain.shape, F32), pltpu.VMEM((3, 2, orb, 8, energies), F32),
            pltpu.VMEM((2, orb, span, energies), BF16), pltpu.SemaphoreType.DMA((orb // 2,))],
        compiler_params=small,
    )(near, move(near_edge, "energy", pair), move(near_edge, "energy", cross), far_first, far_join, w_near, w_far, own, table, gn, gd)
    return result.reshape(bare_green.shape)


def solution(mesh):
    placed = (
        P(None, None, None, "atom", "energy"),
        P(None, None, None, "atom"),
        P("atom", None),
        P(),
        P(),
        P(),
    )
    return jax.shard_map(
        per_device,
        mesh=mesh,
        in_specs=placed,
        out_specs=P(None, None, None, "atom", "energy"),
        check_vma=False,
    )
```

```python
import functools
import math
import jax
import jax.numpy as jnp
from jax import lax
from jax.experimental import pallas as pl
from jax.experimental.pallas import tpu as pltpu
from jax.sharding import PartitionSpec as P

WIDTH = 4
EDGE = 2 * WIDTH
LANES = 128
F32 = jnp.float32
BF16 = jnp.bfloat16


def iota(shape, axis):
    return lax.broadcasted_iota(jnp.int32, shape, axis)


def dot(a, b, dims=((1,), (0,))):
    return lax.dot_general(a, b, (dims, ((), ())), preferred_element_type=F32)


def steps_below(x, step, most):
    return sum((x >= step * m).astype(jnp.int32) for m in range(1, most))


def pack_edges(orb, g_ref, edge_ref):
    span = g_ref.shape[1] // orb
    lane = iota((span, LANES), 1)
    for r in range(2):
        total = jnp.zeros((span, LANES), F32)
        for k in range(orb):
            x = g_ref[r, k * span:(k + 1) * span].astype(F32)
            turned = pltpu.roll(x, EDGE * k + WIDTH, 1)
            total = jnp.where((lane >= EDGE * k) & (lane < EDGE * (k + 1)), turned, total)
        edge_ref[r * span:(r + 1) * span] = total.astype(BF16)


def from_sides(pair_ref, cross_ref):
    below = ((iota(pair_ref.shape, 1) & WIDTH) == 0) ^ ((lax.axis_index("energy") & 1) == 0)
    return jnp.where(below, pair_ref[...].astype(F32), cross_ref[...].astype(F32)).astype(BF16)


def pack_kernel(orb, g_hbm, c_hbm, nbr_hbm, sh_hbm, st_hbm, oc_hbm,
                edge_ref, g_ref, c_ref, near_ref, sh_ref, st_ref, oc_ref, nbr_ref, sems):
    ends = ((g_hbm, g_ref), (nbr_hbm, nbr_ref), (c_hbm, c_ref), (sh_hbm, sh_ref), (st_hbm, st_ref), (oc_hbm, oc_ref))
    copies = [pltpu.make_async_copy(source, target, sems.at[i]) for i, (source, target) in enumerate(ends)]
    for copy in copies:
        copy.start()
    copies[0].wait()
    pack_edges(orb, g_ref, edge_ref)
    copies[1].wait()
    atoms, bonds = nbr_ref.shape
    own = iota(near_ref.shape[1:], 0) & (atoms - 1)
    for n in range(bonds):
        near = jnp.zeros(near_ref.shape[1:], jnp.int32)
        for a in range(atoms):
            near = jnp.where(own == a, nbr_ref[a, n], near)
        near_ref[n] = near
    for copy in copies[2:]:
        copy.wait()


def join_kernel(pair_ref, cross_ref, g_ref, after_ref, out_ref, rim_ref):
    rows = g_ref.shape[1]
    rim = pair_ref.shape[0]
    rest = (out_ref.shape[0] - rim) // 2
    for r in range(2):
        out_ref[r * rest:(r + 1) * rest] = g_ref[r, rows - rest:]
    halo = from_sides(pair_ref, cross_ref)
    out_ref[2 * rest:] = halo
    rim_ref[...] = halo


def pass_kernel(orb, x_ref, after_ref, out_ref, edge_ref):
    out_ref[...] = x_ref[:, :out_ref.shape[1]]
    pack_edges(orb, x_ref, edge_ref)


def band_weights(sh_ref, st_ref, oc_ref):
    shifts = sh_ref[...]
    emit = st_ref[...] * oc_ref[...]
    absorb = st_ref[...] * (oc_ref[...] + 1.0)
    zero = jnp.zeros_like(emit)
    weights = []
    for o in range(-WIDTH, WIDTH + 1):
        both = jnp.where(shifts == -o, emit, zero) + jnp.where(shifts == o, absorb, zero)
        weights.append(jnp.sum(both, axis=1, keepdims=True))
    return weights


def banded(weights, gap, keep=None):
    table = jnp.zeros(gap.shape, F32)
    for o in range(-WIDTH, WIDTH + 1):
        hit = gap == o
        if keep is not None:
            hit = hit & keep
        table = jnp.where(hit, weights[o + WIDTH], table)
    return table.astype(BF16)


def factors_kernel(orb, atoms, c_ref, near_ref, sh_ref, st_ref, oc_ref, t1_ref, t2_ref, table_ref):
    bonds = near_ref.shape[0]
    energies = table_ref.shape[2]
    span = orb * atoms
    cols = t1_ref.shape[3]
    period = t2_ref.shape[4]
    here = lax.axis_index("atom")
    place = lax.axis_index("energy")
    last = lax.axis_size("energy") - 1

    weights = band_weights(sh_ref, st_ref, oc_ref)
    band = banded(weights, iota((energies, energies), 0) - iota((energies, energies), 1))
    rim = (LANES, energies)
    row = iota(rim, 0)
    spot = row & (EDGE - 1)
    below = spot < WIDTH
    keep = jnp.where(below, jnp.where(place > 0, 1, 0), jnp.where(place < last, 1, 0)) > 0
    edge = banded(weights, jnp.where(below, spot - WIDTH, spot - WIDTH + energies) - iota(rim, 1), keep)
    for k in range(orb):
        table_ref[k, :energies] = band
        table_ref[k, energies:] = jnp.where((row >= EDGE * k) & (row < EDGE * (k + 1)), edge, jnp.zeros_like(edge))

    c = c_ref[...]
    krow, klane = iota((orb, cols), 0), iota((orb, cols), 1)
    spread = ((klane >= krow * span) & (klane < (krow + 1) * span)).astype(F32).astype(BF16)
    left = dot(c, spread).reshape(bonds * orb * atoms // 8, 8, cols)
    turned = pltpu.roll(left, atoms, 1)
    upper = iota(left.shape, 1) < atoms
    first = jnp.where(upper, left, turned)
    second = jnp.where(upper, turned, left)
    both = jnp.stack([first, second], axis=1).reshape(bonds, orb, 8, cols)
    t1_ref[...] = jnp.concatenate([both, both], axis=2).astype(BF16)

    lrow, llane = iota((orb, period), 0), iota((orb, period), 1)
    inner = llane - span * steps_below(llane, span, period // span)
    spread = ((inner >= lrow * atoms) & (inner < (lrow + 1) * atoms)).astype(F32).astype(BF16)
    right = dot(c, spread).reshape(bonds, span // 16, 16, period)
    odd = here & 1
    base = (here + 1 - 2 * odd, here, here - 1 + 2 * odd)
    other = iota((16, period), 1) & (atoms - 1)
    for n in range(bonds):
        near = jnp.concatenate([near_ref[n]] * (period // LANES), axis=1)
        for s in range(3):
            mask = near == other + base[s] * atoms
            t2_ref[s, n] = jnp.where(mask[None], right[n], 0.0).astype(BF16)


def weights_kernel(orb, atoms, t1_ref, t2_ref, g_ref, wn_ref, wo_ref, gn_ref, gd_ref):
    gr = g_ref[0].astype(F32)
    gi = g_ref[1].astype(F32)
    for c, x in enumerate((gr, gi, gr + gi)):
        gn_ref[c] = x.reshape(gn_ref.shape[1:])
        gd_ref[c] = doubled(x, orb, atoms)
    fill(t1_ref, t2_ref, (wn_ref, wo_ref), 0)


def others_kernel(orb, t1_ref, t2_ref, table_ref, g_ref, rim_ref, wo_ref, wf_ref, s_ref):
    fill(t1_ref, t2_ref, (wf_ref,), 2)
    s_ref[...] = slab_products([wo_ref], [whole(g_ref, orb)], [rim_ref[...]], table_ref)


def fill(t1_ref, t2_ref, outs, first):
    bonds, orb = t1_ref.shape[:2]
    groups, period = t2_ref.shape[2], t2_ref.shape[4]
    for t in range(t1_ref.shape[3] // LANES):
        at = slice(t * LANES, (t + 1) * LANES)
        start = (t * LANES) % period
        cut = slice(start, start + LANES)
        for s, out in enumerate(outs):
            held = [[t2_ref[s + first, n, q, :, cut] for n in range(bonds)] for q in range(groups)]

            def body(i, carry):
                x = [t1_ref[n, i, :, at] for n in range(bonds)]
                for q in range(groups):
                    terms = [x[n] * held[q][n] for n in range(bonds)]
                    while len(terms) > 1:
                        pairs = [terms[n] + terms[n + 1] for n in range(0, len(terms) - 1, 2)]
                        terms = pairs + terms[2 * len(pairs):]
                    out[i, q * 16:(q + 1) * 16, at] = terms[0]
                return carry

            lax.fori_loop(0, orb, body, 0, unroll=orb)


def rim_of(join_ref, span):
    return join_ref[join_ref.shape[0] - 2 * span:]


def whole(ref, orb):
    return [[(ref.at[0], k), (ref.at[1], k)] for k in range(orb)]


def joined(parts, join_ref, orb, span):
    blocks = []
    for ref in parts:
        blocks += [[(ref.at[0], k), (ref.at[1], k)] for k in range(ref.shape[1] // span)]
    late = orb - len(blocks)
    return blocks + [[(join_ref, k), (join_ref, late + k)] for k in range(late)]


def slab_products(w_refs, slabs, rims, table_ref):
    orb = len(slabs[0])
    span = rims[0].shape[0] // 2
    rims = jnp.concatenate(rims, axis=0)
    summed = []
    for k in range(orb):
        body = jnp.concatenate([ref[i * span:(i + 1) * span] for slab in slabs for ref, i in slab[k]], axis=0)
        summed.append(dot(jnp.concatenate([body, rims], axis=1), table_ref[k]).astype(BF16))
    total = None
    for s, w_ref in enumerate(w_refs):
        at = 2 * s * span
        right = jnp.concatenate(
            [jnp.concatenate([x[at:at + span], x[at + span:at + 2 * span]], axis=1) for x in summed], axis=0)
        rows = right.shape[0]
        w = w_ref[...].reshape(rows, w_ref.shape[2])[:, :rows]
        part = dot(w, right)
        total = part if total is None else total + part
    return total


def doubled(x, orb, atoms):
    pairs = x.reshape(orb * orb * atoms // 8, 8, x.shape[1])
    turned = pltpu.roll(pairs, atoms, 1)
    upper = iota(pairs.shape, 1) < atoms
    first = jnp.where(upper, pairs, turned)
    second = jnp.where(upper, turned, pairs)
    return jnp.stack([first, second], axis=1).reshape(orb, orb, 8, x.shape[1])


def final_kernel(orb, atoms, near_ref, pair_ref, cross_ref, ff_ref, fj_ref, wn_ref, wf_ref, s_ref, table_ref, gn_ref, gd_ref,
                 out_hbm, sn_ref, ld_ref, out_ref, sems):
    energies = table_ref.shape[2]
    span = orb * atoms
    groups = span // 8
    slabs = [whole(near_ref, orb), joined((ff_ref,), fj_ref, orb, span)]
    rims = [from_sides(pair_ref, cross_ref), rim_of(fj_ref, span)]
    total = s_ref[...] + slab_products([wn_ref, wf_ref], slabs, rims, table_ref)
    re, im = total[:, :energies], total[:, energies:]
    for c, x in enumerate((re, im, re + im)):
        sn_ref[c] = x.reshape(orb, groups, 8, energies)

    def product(left, right_ref, acc):
        for k in range(orb):
            for c in range(3):
                right = right_ref[c, k]
                for d in range(2):
                    term = left(c, d, k)[None] * right
                    acc[c][d] = term if acc[c][d] is None else acc[c][d] + term
        return acc

    def sent(p):
        at = pl.ds(2 * p, 2)
        return pltpu.make_async_copy(out_ref.at[:, at], out_hbm.at[:, at], sems.at[p])

    def pair(p, carry):
        m = product(lambda c, d, k: gd_ref[c, 2 * p + d, k], sn_ref, [[None, None] for _ in range(3)])
        upper = iota((groups, 8, energies), 1) < atoms
        for d in range(2):
            lr = m[0][d] - m[1][d]
            li = m[2][d] - (m[0][d] + m[1][d])
            for c, x in enumerate((lr, li, lr + li)):
                turned = pltpu.roll(x, atoms, 1)
                first = jnp.where(upper, x, turned)
                second = jnp.where(upper, turned, x)
                ld_ref[c, d] = jnp.stack([first, second], axis=1).reshape(orb, 8, energies)
        m = product(lambda c, d, k: ld_ref[c, d, k], gn_ref, [[None, None] for _ in range(3)])
        for d in range(2):
            i = 2 * p + d
            ur = gn_ref[0, i] + (m[0][d] - m[1][d])
            ui = gn_ref[1, i] + (m[2][d] - (m[0][d] + m[1][d]))
            out_ref[0, i] = ur.reshape(orb * atoms, energies).astype(BF16)
            out_ref[1, i] = ui.reshape(orb * atoms, energies).astype(BF16)
        sent(p).start()
        return carry

    lax.fori_loop(0, orb // 2, pair, 0, unroll=1)
    for p in range(orb // 2):
        sent(p).wait()


def move(value, axis, target):
    count = lax.axis_size(axis)
    return lax.ppermute(value, axis, [(i, target(i) % count) for i in range(count)])


def pair(i):
    return i ^ 1


def cross(i):
    return i + 1 if i & 1 else i - 1


def relay(i, count):
    if i & 1:
        return i - 2 if i > 1 else 0
    return i + 2 if i + 2 < count else count - 1


def move_far(value):
    atoms, energies = lax.axis_size("atom"), lax.axis_size("energy")
    moves = []
    for a in range(atoms):
        b = a + 1 if a & 1 else a - 1
        for e in range(energies):
            target = (b, e) if 0 <= b < atoms else (a, (e ^ 1) % energies)
            moves.append((a * energies + e, target[0] * energies + target[1]))
    return lax.ppermute(value, ("atom", "energy"), moves)


def per_device(bare_green, coupling_grad, neighbours, shifts, strength, occupation):
    _, orb, _, atoms, energies = bare_green.shape
    bonds = coupling_grad.shape[0]
    rows = orb * orb * atoms
    span = orb * atoms
    cols = -(-rows // LANES) * LANES
    period = span * LANES // math.gcd(span, LANES)
    early = orb // 2
    late = 2 * (orb - early) * span + 2 * span
    vmem = pl.BlockSpec(memory_space=pltpu.VMEM)
    smem = pl.BlockSpec(memory_space=pltpu.SMEM)
    small = pltpu.CompilerParams(vmem_limit_bytes=20 * 1024 * 1024)

    def shape(*dims, kind=BF16):
        return jax.ShapeDtypeStruct(dims, kind)

    def call(kernel, name, out_shape, *operands, scratch=(), scalars=()):
        return pl.pallas_call(
            kernel, out_shape=out_shape, name=name,
            in_specs=[smem if i in scalars else vmem for i in range(len(operands))],
            out_specs=jax.tree.map(lambda _: vmem, out_shape),
            scratch_shapes=scratch, compiler_params=small,
        )(*operands)

    green = bare_green.reshape(2, rows, energies)
    near = move(green, "atom", pair)
    grads = jnp.transpose(coupling_grad, (0, 1, 3, 2)).reshape(bonds * orb * atoms, orb)
    phonons = [x[None] for x in (shifts, strength, occupation)]
    fetched = [pltpu.with_memory_space_constraint(x, pltpu.HBM) for x in (green, grads, neighbours, *phonons)]
    edge, held, grads, near_atoms, *phonons = pl.pallas_call(
        functools.partial(pack_kernel, orb), name="pack",
        out_shape=[shape(2 * span, LANES), shape(2, rows, energies), shape(*grads.shape),
                   shape(bonds, 16, LANES, kind=jnp.int32)] + [shape(*x.shape, kind=x.dtype) for x in phonons],
        in_specs=[pl.BlockSpec(memory_space=pltpu.HBM)] * 6, out_specs=[vmem] * 7,
        scratch_shapes=[pltpu.SMEM(neighbours.shape, jnp.int32), pltpu.SemaphoreType.DMA((6,))],
        compiler_params=small,
    )(*fetched)
    left, right, table = call(
        functools.partial(factors_kernel, orb, atoms), "factors",
        [shape(bonds, orb, 16, cols), shape(3, bonds, span // 16, 16, period),
         shape(orb, energies + LANES, energies)],
        grads, near_atoms, *phonons)
    weight = shape(orb, span, cols)
    plain = shape(3, orb, span // 8, 8, energies, kind=F32)
    w_near, w_own, gn, gd = call(
        functools.partial(weights_kernel, orb, atoms), "weights",
        [weight, weight, plain, shape(3, orb, orb, 8, energies, kind=F32)], left, right, held)
    join, rim = call(
        join_kernel, "join", [shape(late, energies), shape(2 * span, LANES)],
        move(edge, "energy", pair), move(edge, "energy", cross), held, w_near)
    far_join = move_far(join)
    passed, near_edge = call(
        functools.partial(pass_kernel, orb), "pack_near",
        [shape(2, early * span, energies), shape(2 * span, LANES)], near, join)
    far_first = move(passed, "atom", lambda i: relay(i, lax.axis_size("atom")))
    w_far, own = call(
        functools.partial(others_kernel, orb), "others", [weight, shape(rows, 2 * energies, kind=F32)],
        left, right, table, held, rim, w_own)

    result = pl.pallas_call(
        functools.partial(final_kernel, orb, atoms), name="green_update",
        out_shape=shape(2, orb, span, energies),
        in_specs=[vmem] * 11, out_specs=pl.BlockSpec(memory_space=pltpu.HBM),
        scratch_shapes=[
            pltpu.VMEM(plain.shape, F32), pltpu.VMEM((3, 2, orb, 8, energies), F32),
            pltpu.VMEM((2, orb, span, energies), BF16), pltpu.SemaphoreType.DMA((orb // 2,))],
        compiler_params=small,
    )(near, move(near_edge, "energy", pair), move(near_edge, "energy", cross), far_first, far_join, w_near, w_far, own, table, gn, gd)
    return result.reshape(bare_green.shape)


def solution(mesh):
    placed = (
        P(None, None, None, "atom", "energy"),
        P(None, None, None, "atom"),
        P("atom", None),
        P(),
        P(),
        P(),
    )
    return jax.shard_map(
        per_device,
        mesh=mesh,
        in_specs=placed,
        out_specs=P(None, None, None, "atom", "energy"),
        check_vma=False,
    )
```

```python
import functools
import math
import jax
import jax.numpy as jnp
from jax import lax
from jax.experimental import pallas as pl
from jax.experimental.pallas import tpu as pltpu
from jax.sharding import PartitionSpec as P

WIDTH = 4
EDGE = 2 * WIDTH
LANES = 128
F32 = jnp.float32
BF16 = jnp.bfloat16


def iota(shape, axis):
    return lax.broadcasted_iota(jnp.int32, shape, axis)


def dot(a, b, dims=((1,), (0,))):
    return lax.dot_general(a, b, (dims, ((), ())), preferred_element_type=F32)


def steps_below(x, step, most):
    return sum((x >= step * m).astype(jnp.int32) for m in range(1, most))


def pack_edges(orb, g_ref, edge_ref):
    span = g_ref.shape[1] // orb
    lane = iota((span, LANES), 1)
    for r in range(2):
        total = jnp.zeros((span, LANES), F32)
        for k in range(orb):
            x = g_ref[r, k * span:(k + 1) * span].astype(F32)
            turned = pltpu.roll(x, EDGE * k + WIDTH, 1)
            total = jnp.where((lane >= EDGE * k) & (lane < EDGE * (k + 1)), turned, total)
        edge_ref[r * span:(r + 1) * span] = total.astype(BF16)


def from_sides(pair_ref, cross_ref):
    below = ((iota(pair_ref.shape, 1) & WIDTH) == 0) ^ ((lax.axis_index("energy") & 1) == 0)
    return jnp.where(below, pair_ref[...].astype(F32), cross_ref[...].astype(F32)).astype(BF16)


def pack_kernel(orb, g_hbm, c_hbm, nbr_hbm, sh_hbm, st_hbm, oc_hbm,
                edge_ref, g_ref, c_ref, near_ref, sh_ref, st_ref, oc_ref, nbr_ref, sems):
    ends = ((g_hbm, g_ref), (nbr_hbm, nbr_ref), (c_hbm, c_ref), (sh_hbm, sh_ref), (st_hbm, st_ref), (oc_hbm, oc_ref))
    copies = [pltpu.make_async_copy(source, target, sems.at[i]) for i, (source, target) in enumerate(ends)]
    for copy in copies:
        copy.start()
    copies[0].wait()
    pack_edges(orb, g_ref, edge_ref)
    copies[1].wait()
    atoms, bonds = nbr_ref.shape
    own = iota(near_ref.shape[1:], 0) & (atoms - 1)
    for n in range(bonds):
        near = jnp.zeros(near_ref.shape[1:], jnp.int32)
        for a in range(atoms):
            near = jnp.where(own == a, nbr_ref[a, n], near)
        near_ref[n] = near
    for copy in copies[2:]:
        copy.wait()


def join_kernel(pair_ref, cross_ref, g_ref, after_ref, out_ref, rim_ref):
    rows = g_ref.shape[1]
    rim = pair_ref.shape[0]
    rest = (out_ref.shape[0] - rim) // 2
    for r in range(2):
        out_ref[r * rest:(r + 1) * rest] = g_ref[r, rows - rest:]
    halo = from_sides(pair_ref, cross_ref)
    out_ref[2 * rest:] = halo
    rim_ref[...] = halo


def pass_kernel(orb, x_ref, after_ref, out_ref, edge_ref):
    out_ref[...] = x_ref[:, :out_ref.shape[1]]
    pack_edges(orb, x_ref, edge_ref)


def band_weights(sh_ref, st_ref, oc_ref):
    shifts = sh_ref[...]
    emit = st_ref[...] * oc_ref[...]
    absorb = st_ref[...] * (oc_ref[...] + 1.0)
    zero = jnp.zeros_like(emit)
    weights = []
    for o in range(-WIDTH, WIDTH + 1):
        both = jnp.where(shifts == -o, emit, zero) + jnp.where(shifts == o, absorb, zero)
        weights.append(jnp.sum(both, axis=1, keepdims=True))
    return weights


def banded(weights, gap, keep=None):
    table = jnp.zeros(gap.shape, F32)
    for o in range(-WIDTH, WIDTH + 1):
        hit = gap == o
        if keep is not None:
            hit = hit & keep
        table = jnp.where(hit, weights[o + WIDTH], table)
    return table.astype(BF16)


def factors_kernel(orb, atoms, c_ref, near_ref, sh_ref, st_ref, oc_ref, t1_ref, t2_ref, table_ref):
    bonds = near_ref.shape[0]
    energies = table_ref.shape[2]
    span = orb * atoms
    cols = t1_ref.shape[3]
    period = t2_ref.shape[4]
    here = lax.axis_index("atom")
    place = lax.axis_index("energy")
    last = lax.axis_size("energy") - 1

    weights = band_weights(sh_ref, st_ref, oc_ref)
    band = banded(weights, iota((energies, energies), 0) - iota((energies, energies), 1))
    rim = (LANES, energies)
    row = iota(rim, 0)
    spot = row & (EDGE - 1)
    below = spot < WIDTH
    keep = jnp.where(below, jnp.where(place > 0, 1, 0), jnp.where(place < last, 1, 0)) > 0
    edge = banded(weights, jnp.where(below, spot - WIDTH, spot - WIDTH + energies) - iota(rim, 1), keep)
    for k in range(orb):
        table_ref[k, :energies] = band
        table_ref[k, energies:] = jnp.where((row >= EDGE * k) & (row < EDGE * (k + 1)), edge, jnp.zeros_like(edge))

    c = c_ref[...]
    krow, klane = iota((orb, cols), 0), iota((orb, cols), 1)
    spread = ((klane >= krow * span) & (klane < (krow + 1) * span)).astype(F32).astype(BF16)
    left = dot(c, spread).reshape(bonds * orb * atoms // 8, 8, cols)
    turned = pltpu.roll(left, atoms, 1)
    upper = iota(left.shape, 1) < atoms
    first = jnp.where(upper, left, turned)
    second = jnp.where(upper, turned, left)
    both = jnp.stack([first, second], axis=1).reshape(bonds, orb, 8, cols)
    t1_ref[...] = jnp.concatenate([both, both], axis=2).astype(BF16)

    lrow, llane = iota((orb, period), 0), iota((orb, period), 1)
    inner = llane - span * steps_below(llane, span, period // span)
    spread = ((inner >= lrow * atoms) & (inner < (lrow + 1) * atoms)).astype(F32).astype(BF16)
    right = dot(c, spread).reshape(bonds, span // 16, 16, period)
    odd = here & 1
    base = (here + 1 - 2 * odd, here, here - 1 + 2 * odd)
    other = iota((16, period), 1) & (atoms - 1)
    for n in range(bonds):
        near = jnp.concatenate([near_ref[n]] * (period // LANES), axis=1)
        for s in range(3):
            mask = near == other + base[s] * atoms
            t2_ref[s, n] = jnp.where(mask[None], right[n], 0.0).astype(BF16)


def weights_kernel(orb, atoms, t1_ref, t2_ref, g_ref, wn_ref, wo_ref, gn_ref, gd_ref):
    gr = g_ref[0].astype(F32)
    gi = g_ref[1].astype(F32)
    for c, x in enumerate((gr, gi, gr + gi)):
        gn_ref[c] = x.reshape(gn_ref.shape[1:])
        gd_ref[c] = doubled(x, orb, atoms)
    fill(t1_ref, t2_ref, (wn_ref, wo_ref), 0)


def far_kernel(t1_ref, t2_ref, after_ref, wf_ref):
    fill(t1_ref, t2_ref, (wf_ref,), 2)


def own_kernel(orb, table_ref, g_ref, rim_ref, wo_ref, s_ref):
    s_ref[...] = slab_products([wo_ref], [whole(g_ref, orb)], [rim_ref[...]], table_ref)


def fill(t1_ref, t2_ref, outs, first):
    bonds, orb = t1_ref.shape[:2]
    groups, period = t2_ref.shape[2], t2_ref.shape[4]
    for t in range(t1_ref.shape[3] // LANES):
        at = slice(t * LANES, (t + 1) * LANES)
        start = (t * LANES) % period
        cut = slice(start, start + LANES)
        for s, out in enumerate(outs):
            held = [[t2_ref[s + first, n, q, :, cut] for n in range(bonds)] for q in range(groups)]

            def body(i, carry):
                x = [t1_ref[n, i, :, at] for n in range(bonds)]
                for q in range(groups):
                    terms = [x[n] * held[q][n] for n in range(bonds)]
                    while len(terms) > 1:
                        pairs = [terms[n] + terms[n + 1] for n in range(0, len(terms) - 1, 2)]
                        terms = pairs + terms[2 * len(pairs):]
                    out[i, q * 16:(q + 1) * 16, at] = terms[0]
                return carry

            lax.fori_loop(0, orb, body, 0, unroll=orb)


def rim_of(join_ref, span):
    return join_ref[join_ref.shape[0] - 2 * span:]


def whole(ref, orb):
    return [[(ref.at[0], k), (ref.at[1], k)] for k in range(orb)]


def joined(parts, join_ref, orb, span):
    blocks = []
    for ref in parts:
        blocks += [[(ref.at[0], k), (ref.at[1], k)] for k in range(ref.shape[1] // span)]
    late = orb - len(blocks)
    return blocks + [[(join_ref, k), (join_ref, late + k)] for k in range(late)]


def slab_products(w_refs, slabs, rims, table_ref):
    orb = len(slabs[0])
    span = rims[0].shape[0] // 2
    rims = jnp.concatenate(rims, axis=0)
    summed = []
    for k in range(orb):
        body = jnp.concatenate([ref[i * span:(i + 1) * span] for slab in slabs for ref, i in slab[k]], axis=0)
        summed.append(dot(jnp.concatenate([body, rims], axis=1), table_ref[k]).astype(BF16))
    total = None
    for s, w_ref in enumerate(w_refs):
        at = 2 * s * span
        right = jnp.concatenate(
            [jnp.concatenate([x[at:at + span], x[at + span:at + 2 * span]], axis=1) for x in summed], axis=0)
        rows = right.shape[0]
        w = w_ref[...].reshape(rows, w_ref.shape[2])[:, :rows]
        part = dot(w, right)
        total = part if total is None else total + part
    return total


def doubled(x, orb, atoms):
    pairs = x.reshape(orb * orb * atoms // 8, 8, x.shape[1])
    turned = pltpu.roll(pairs, atoms, 1)
    upper = iota(pairs.shape, 1) < atoms
    first = jnp.where(upper, pairs, turned)
    second = jnp.where(upper, turned, pairs)
    return jnp.stack([first, second], axis=1).reshape(orb, orb, 8, x.shape[1])


def final_kernel(orb, atoms, near_ref, pair_ref, cross_ref, ff_ref, fj_ref, wn_ref, wf_ref, s_ref, table_ref, gn_ref, gd_ref,
                 out_hbm, sn_ref, ld_ref, out_ref, sems):
    energies = table_ref.shape[2]
    span = orb * atoms
    groups = span // 8
    slabs = [whole(near_ref, orb), joined((ff_ref,), fj_ref, orb, span)]
    rims = [from_sides(pair_ref, cross_ref), rim_of(fj_ref, span)]
    total = s_ref[...] + slab_products([wn_ref, wf_ref], slabs, rims, table_ref)
    re, im = total[:, :energies], total[:, energies:]
    for c, x in enumerate((re, im, re + im)):
        sn_ref[c] = x.reshape(orb, groups, 8, energies)

    def product(left, right_ref, acc):
        for k in range(orb):
            for c in range(3):
                right = right_ref[c, k]
                for d in range(2):
                    term = left(c, d, k)[None] * right
                    acc[c][d] = term if acc[c][d] is None else acc[c][d] + term
        return acc

    def sent(p):
        at = pl.ds(2 * p, 2)
        return pltpu.make_async_copy(out_ref.at[:, at], out_hbm.at[:, at], sems.at[p])

    def pair(p, carry):
        m = product(lambda c, d, k: gd_ref[c, 2 * p + d, k], sn_ref, [[None, None] for _ in range(3)])
        upper = iota((groups, 8, energies), 1) < atoms
        for d in range(2):
            lr = m[0][d] - m[1][d]
            li = m[2][d] - (m[0][d] + m[1][d])
            for c, x in enumerate((lr, li, lr + li)):
                turned = pltpu.roll(x, atoms, 1)
                first = jnp.where(upper, x, turned)
                second = jnp.where(upper, turned, x)
                ld_ref[c, d] = jnp.stack([first, second], axis=1).reshape(orb, 8, energies)
        m = product(lambda c, d, k: ld_ref[c, d, k], gn_ref, [[None, None] for _ in range(3)])
        for d in range(2):
            i = 2 * p + d
            ur = gn_ref[0, i] + (m[0][d] - m[1][d])
            ui = gn_ref[1, i] + (m[2][d] - (m[0][d] + m[1][d]))
            out_ref[0, i] = ur.reshape(orb * atoms, energies).astype(BF16)
            out_ref[1, i] = ui.reshape(orb * atoms, energies).astype(BF16)
        sent(p).start()
        return carry

    lax.fori_loop(0, orb // 2, pair, 0, unroll=1)
    for p in range(orb // 2):
        sent(p).wait()


def move(value, axis, target):
    count = lax.axis_size(axis)
    return lax.ppermute(value, axis, [(i, target(i) % count) for i in range(count)])


def pair(i):
    return i ^ 1


def cross(i):
    return i + 1 if i & 1 else i - 1


def relay(i, count):
    if i & 1:
        return i - 2 if i > 1 else 0
    return i + 2 if i + 2 < count else count - 1


def move_far(value):
    atoms, energies = lax.axis_size("atom"), lax.axis_size("energy")
    moves = []
    for a in range(atoms):
        b = a + 1 if a & 1 else a - 1
        for e in range(energies):
            target = (b, e) if 0 <= b < atoms else (a, (e ^ 1) % energies)
            moves.append((a * energies + e, target[0] * energies + target[1]))
    return lax.ppermute(value, ("atom", "energy"), moves)


def per_device(bare_green, coupling_grad, neighbours, shifts, strength, occupation):
    _, orb, _, atoms, energies = bare_green.shape
    bonds = coupling_grad.shape[0]
    rows = orb * orb * atoms
    span = orb * atoms
    cols = -(-rows // LANES) * LANES
    period = span * LANES // math.gcd(span, LANES)
    early = orb // 3
    late = 2 * (orb - early) * span + 2 * span
    vmem = pl.BlockSpec(memory_space=pltpu.VMEM)
    smem = pl.BlockSpec(memory_space=pltpu.SMEM)
    small = pltpu.CompilerParams(vmem_limit_bytes=20 * 1024 * 1024)

    def shape(*dims, kind=BF16):
        return jax.ShapeDtypeStruct(dims, kind)

    def call(kernel, name, out_shape, *operands, scratch=(), scalars=()):
        return pl.pallas_call(
            kernel, out_shape=out_shape, name=name,
            in_specs=[smem if i in scalars else vmem for i in range(len(operands))],
            out_specs=jax.tree.map(lambda _: vmem, out_shape),
            scratch_shapes=scratch, compiler_params=small,
        )(*operands)

    green = bare_green.reshape(2, rows, energies)
    near = move(green, "atom", pair)
    grads = jnp.transpose(coupling_grad, (0, 1, 3, 2)).reshape(bonds * orb * atoms, orb)
    phonons = [x[None] for x in (shifts, strength, occupation)]
    fetched = [pltpu.with_memory_space_constraint(x, pltpu.HBM) for x in (green, grads, neighbours, *phonons)]
    edge, held, grads, near_atoms, *phonons = pl.pallas_call(
        functools.partial(pack_kernel, orb), name="pack",
        out_shape=[shape(2 * span, LANES), shape(2, rows, energies), shape(*grads.shape),
                   shape(bonds, 16, LANES, kind=jnp.int32)] + [shape(*x.shape, kind=x.dtype) for x in phonons],
        in_specs=[pl.BlockSpec(memory_space=pltpu.HBM)] * 6, out_specs=[vmem] * 7,
        scratch_shapes=[pltpu.SMEM(neighbours.shape, jnp.int32), pltpu.SemaphoreType.DMA((6,))],
        compiler_params=small,
    )(*fetched)
    left, right, table = call(
        functools.partial(factors_kernel, orb, atoms), "factors",
        [shape(bonds, orb, 16, cols), shape(3, bonds, span // 16, 16, period),
         shape(orb, energies + LANES, energies)],
        grads, near_atoms, *phonons)
    weight = shape(orb, span, cols)
    plain = shape(3, orb, span // 8, 8, energies, kind=F32)
    w_near, w_own, gn, gd = call(
        functools.partial(weights_kernel, orb, atoms), "weights",
        [weight, weight, plain, shape(3, orb, orb, 8, energies, kind=F32)], left, right, held)
    join, rim = call(
        join_kernel, "join", [shape(late, energies), shape(2 * span, LANES)],
        move(edge, "energy", pair), move(edge, "energy", cross), held, w_near)
    far_join = move_far(join)
    w_far = call(far_kernel, "far_weights", weight, left, right, join)
    passed, near_edge = call(
        functools.partial(pass_kernel, orb), "pack_near",
        [shape(2, early * span, energies), shape(2 * span, LANES)], near, w_far)
    far_first = move(passed, "atom", lambda i: relay(i, lax.axis_size("atom")))
    own = call(
        functools.partial(own_kernel, orb), "own", shape(rows, 2 * energies, kind=F32), table, held, rim, w_own)

    result = pl.pallas_call(
        functools.partial(final_kernel, orb, atoms), name="green_update",
        out_shape=shape(2, orb, span, energies),
        in_specs=[vmem] * 11, out_specs=pl.BlockSpec(memory_space=pltpu.HBM),
        scratch_shapes=[
            pltpu.VMEM(plain.shape, F32), pltpu.VMEM((3, 2, orb, 8, energies), F32),
            pltpu.VMEM((2, orb, span, energies), BF16), pltpu.SemaphoreType.DMA((orb // 2,))],
        compiler_params=small,
    )(near, move(near_edge, "energy", pair), move(near_edge, "energy", cross), far_first, far_join, w_near, w_far, own, table, gn, gd)
    return result.reshape(bare_green.shape)


def solution(mesh):
    placed = (
        P(None, None, None, "atom", "energy"),
        P(None, None, None, "atom"),
        P("atom", None),
        P(),
        P(),
        P(),
    )
    return jax.shard_map(
        per_device,
        mesh=mesh,
        in_specs=placed,
        out_specs=P(None, None, None, "atom", "energy"),
        check_vma=False,
    )
```

```python
import functools
import math
import jax
import jax.numpy as jnp
from jax import lax
from jax.experimental import pallas as pl
from jax.experimental.pallas import tpu as pltpu
from jax.sharding import PartitionSpec as P

WIDTH = 4
EDGE = 2 * WIDTH
LANES = 128
F32 = jnp.float32
BF16 = jnp.bfloat16


def iota(shape, axis):
    return lax.broadcasted_iota(jnp.int32, shape, axis)


def dot(a, b, dims=((1,), (0,))):
    return lax.dot_general(a, b, (dims, ((), ())), preferred_element_type=F32)


def steps_below(x, step, most):
    return sum((x >= step * m).astype(jnp.int32) for m in range(1, most))


def pack_edges(orb, g_ref, edge_ref):
    span = g_ref.shape[1] // orb
    lane = iota((span, LANES), 1)
    for r in range(2):
        total = jnp.zeros((span, LANES), F32)
        for k in range(orb):
            x = g_ref[r, k * span:(k + 1) * span].astype(F32)
            turned = pltpu.roll(x, EDGE * k + WIDTH, 1)
            total = jnp.where((lane >= EDGE * k) & (lane < EDGE * (k + 1)), turned, total)
        edge_ref[r * span:(r + 1) * span] = total.astype(BF16)


def from_sides(pair_ref, cross_ref):
    below = ((iota(pair_ref.shape, 1) & WIDTH) == 0) ^ ((lax.axis_index("energy") & 1) == 0)
    return jnp.where(below, pair_ref[...].astype(F32), cross_ref[...].astype(F32)).astype(BF16)


def pack_kernel(orb, g_hbm, c_hbm, nbr_hbm, sh_hbm, st_hbm, oc_hbm,
                edge_ref, g_ref, c_ref, near_ref, sh_ref, st_ref, oc_ref, nbr_ref, sems):
    ends = ((g_hbm, g_ref), (nbr_hbm, nbr_ref), (c_hbm, c_ref), (sh_hbm, sh_ref), (st_hbm, st_ref), (oc_hbm, oc_ref))
    copies = [pltpu.make_async_copy(source, target, sems.at[i]) for i, (source, target) in enumerate(ends)]
    for copy in copies:
        copy.start()
    copies[0].wait()
    pack_edges(orb, g_ref, edge_ref)
    copies[1].wait()
    atoms, bonds = nbr_ref.shape
    own = iota(near_ref.shape[1:], 0) & (atoms - 1)
    for n in range(bonds):
        near = jnp.zeros(near_ref.shape[1:], jnp.int32)
        for a in range(atoms):
            near = jnp.where(own == a, nbr_ref[a, n], near)
        near_ref[n] = near
    for copy in copies[2:]:
        copy.wait()


def join_kernel(pair_ref, cross_ref, g_ref, after_ref, out_ref, rim_ref):
    rows = g_ref.shape[1]
    rim = pair_ref.shape[0]
    rest = (out_ref.shape[0] - rim) // 2
    for r in range(2):
        out_ref[r * rest:(r + 1) * rest] = g_ref[r, rows - rest:]
    halo = from_sides(pair_ref, cross_ref)
    out_ref[2 * rest:] = halo
    rim_ref[...] = halo


def pass_kernel(orb, x_ref, after_ref, out_ref, edge_ref):
    out_ref[...] = x_ref[:, :out_ref.shape[1]]
    pack_edges(orb, x_ref, edge_ref)


def band_weights(sh_ref, st_ref, oc_ref):
    shifts = sh_ref[...]
    emit = st_ref[...] * oc_ref[...]
    absorb = st_ref[...] * (oc_ref[...] + 1.0)
    zero = jnp.zeros_like(emit)
    weights = []
    for o in range(-WIDTH, WIDTH + 1):
        both = jnp.where(shifts == -o, emit, zero) + jnp.where(shifts == o, absorb, zero)
        weights.append(jnp.sum(both, axis=1, keepdims=True))
    return weights


def banded(weights, gap, keep=None):
    table = jnp.zeros(gap.shape, F32)
    for o in range(-WIDTH, WIDTH + 1):
        hit = gap == o
        if keep is not None:
            hit = hit & keep
        table = jnp.where(hit, weights[o + WIDTH], table)
    return table.astype(BF16)


def factors_kernel(orb, atoms, c_ref, near_ref, sh_ref, st_ref, oc_ref, t1_ref, t2_ref, table_ref):
    bonds = near_ref.shape[0]
    energies = table_ref.shape[2]
    span = orb * atoms
    cols = t1_ref.shape[3]
    period = t2_ref.shape[4]
    here = lax.axis_index("atom")
    place = lax.axis_index("energy")
    last = lax.axis_size("energy") - 1

    weights = band_weights(sh_ref, st_ref, oc_ref)
    band = banded(weights, iota((energies, energies), 0) - iota((energies, energies), 1))
    rim = (LANES, energies)
    row = iota(rim, 0)
    spot = row & (EDGE - 1)
    below = spot < WIDTH
    keep = jnp.where(below, jnp.where(place > 0, 1, 0), jnp.where(place < last, 1, 0)) > 0
    edge = banded(weights, jnp.where(below, spot - WIDTH, spot - WIDTH + energies) - iota(rim, 1), keep)
    for k in range(orb):
        table_ref[k, :energies] = band
        table_ref[k, energies:] = jnp.where((row >= EDGE * k) & (row < EDGE * (k + 1)), edge, jnp.zeros_like(edge))

    c = c_ref[...]
    krow, klane = iota((orb, cols), 0), iota((orb, cols), 1)
    spread = ((klane >= krow * span) & (klane < (krow + 1) * span)).astype(F32).astype(BF16)
    left = dot(c, spread).reshape(bonds * orb * atoms // 8, 8, cols)
    turned = pltpu.roll(left, atoms, 1)
    upper = iota(left.shape, 1) < atoms
    first = jnp.where(upper, left, turned)
    second = jnp.where(upper, turned, left)
    both = jnp.stack([first, second], axis=1).reshape(bonds, orb, 8, cols)
    t1_ref[...] = jnp.concatenate([both, both], axis=2).astype(BF16)

    lrow, llane = iota((orb, period), 0), iota((orb, period), 1)
    inner = llane - span * steps_below(llane, span, period // span)
    spread = ((inner >= lrow * atoms) & (inner < (lrow + 1) * atoms)).astype(F32).astype(BF16)
    right = dot(c, spread).reshape(bonds, span // 16, 16, period)
    odd = here & 1
    base = (here + 1 - 2 * odd, here, here - 1 + 2 * odd)
    other = iota((16, period), 1) & (atoms - 1)
    for n in range(bonds):
        near = jnp.concatenate([near_ref[n]] * (period // LANES), axis=1)
        for s in range(3):
            mask = near == other + base[s] * atoms
            t2_ref[s, n] = jnp.where(mask[None], right[n], 0.0).astype(BF16)


def weights_kernel(orb, atoms, t1_ref, t2_ref, g_ref, wn_ref, wo_ref, gn_ref, gd_ref):
    gr = g_ref[0].astype(F32)
    gi = g_ref[1].astype(F32)
    for c, x in enumerate((gr, gi, gr + gi)):
        gn_ref[c] = x.reshape(gn_ref.shape[1:])
        gd_ref[c] = doubled(x, orb, atoms)
    fill(t1_ref, t2_ref, (wn_ref, wo_ref), 0)


def far_kernel(t1_ref, t2_ref, after_ref, wf_ref):
    fill(t1_ref, t2_ref, (wf_ref,), 2)


def own_kernel(orb, table_ref, g_ref, rim_ref, wo_ref, s_ref):
    s_ref[...] = slab_products([wo_ref], [whole(g_ref, orb)], [rim_ref[...]], table_ref)


def fill(t1_ref, t2_ref, outs, first):
    bonds, orb = t1_ref.shape[:2]
    groups, period = t2_ref.shape[2], t2_ref.shape[4]
    for t in range(t1_ref.shape[3] // LANES):
        at = slice(t * LANES, (t + 1) * LANES)
        start = (t * LANES) % period
        cut = slice(start, start + LANES)
        for s, out in enumerate(outs):
            held = [[t2_ref[s + first, n, q, :, cut] for n in range(bonds)] for q in range(groups)]

            def body(i, carry):
                x = [t1_ref[n, i, :, at] for n in range(bonds)]
                for q in range(groups):
                    terms = [x[n] * held[q][n] for n in range(bonds)]
                    while len(terms) > 1:
                        pairs = [terms[n] + terms[n + 1] for n in range(0, len(terms) - 1, 2)]
                        terms = pairs + terms[2 * len(pairs):]
                    out[i, q * 16:(q + 1) * 16, at] = terms[0]
                return carry

            lax.fori_loop(0, orb, body, 0, unroll=orb)


def rim_of(join_ref, span):
    return join_ref[join_ref.shape[0] - 2 * span:]


def whole(ref, orb):
    return [[(ref.at[0], k), (ref.at[1], k)] for k in range(orb)]


def joined(parts, join_ref, orb, span):
    blocks = []
    for ref in parts:
        blocks += [[(ref.at[0], k), (ref.at[1], k)] for k in range(ref.shape[1] // span)]
    late = orb - len(blocks)
    return blocks + [[(join_ref, k), (join_ref, late + k)] for k in range(late)]


def slab_products(w_refs, slabs, rims, table_ref):
    orb = len(slabs[0])
    span = rims[0].shape[0] // 2
    rims = jnp.concatenate(rims, axis=0)
    summed = []
    for k in range(orb):
        body = jnp.concatenate([ref[i * span:(i + 1) * span] for slab in slabs for ref, i in slab[k]], axis=0)
        summed.append(dot(jnp.concatenate([body, rims], axis=1), table_ref[k]).astype(BF16))
    total = None
    for s, w_ref in enumerate(w_refs):
        at = 2 * s * span
        right = jnp.concatenate(
            [jnp.concatenate([x[at:at + span], x[at + span:at + 2 * span]], axis=1) for x in summed], axis=0)
        rows = right.shape[0]
        w = w_ref[...].reshape(rows, w_ref.shape[2])[:, :rows]
        part = dot(w, right)
        total = part if total is None else total + part
    return total


def doubled(x, orb, atoms):
    pairs = x.reshape(orb * orb * atoms // 8, 8, x.shape[1])
    turned = pltpu.roll(pairs, atoms, 1)
    upper = iota(pairs.shape, 1) < atoms
    first = jnp.where(upper, pairs, turned)
    second = jnp.where(upper, turned, pairs)
    return jnp.stack([first, second], axis=1).reshape(orb, orb, 8, x.shape[1])


def final_kernel(orb, atoms, near_ref, pair_ref, cross_ref, ff_ref, fj_ref, wn_ref, wf_ref, s_ref, table_ref, gn_ref, gd_ref,
                 out_hbm, sn_ref, ld_ref, out_ref, sems):
    energies = table_ref.shape[2]
    span = orb * atoms
    groups = span // 8
    slabs = [whole(near_ref, orb), joined((ff_ref,), fj_ref, orb, span)]
    rims = [from_sides(pair_ref, cross_ref), rim_of(fj_ref, span)]
    total = s_ref[...] + slab_products([wn_ref, wf_ref], slabs, rims, table_ref)
    re, im = total[:, :energies], total[:, energies:]
    for c, x in enumerate((re, im, re + im)):
        sn_ref[c] = x.reshape(orb, groups, 8, energies)

    def product(left, right_ref, acc):
        for k in range(orb):
            for c in range(3):
                right = right_ref[c, k]
                for d in range(2):
                    term = left(c, d, k)[None] * right
                    acc[c][d] = term if acc[c][d] is None else acc[c][d] + term
        return acc

    def sent(p):
        at = pl.ds(2 * p, 2)
        return pltpu.make_async_copy(out_ref.at[:, at], out_hbm.at[:, at], sems.at[p])

    def pair(p, carry):
        m = product(lambda c, d, k: gd_ref[c, 2 * p + d, k], sn_ref, [[None, None] for _ in range(3)])
        upper = iota((groups, 8, energies), 1) < atoms
        for d in range(2):
            lr = m[0][d] - m[1][d]
            li = m[2][d] - (m[0][d] + m[1][d])
            rows = []
            for x in (lr, li):
                turned = pltpu.roll(x, atoms, 1)
                first = jnp.where(upper, x, turned)
                second = jnp.where(upper, turned, x)
                rows.append(jnp.stack([first, second], axis=1).reshape(orb, 8, energies))
            for c, x in enumerate((rows[0], rows[1], rows[0] + rows[1])):
                ld_ref[c, d] = x
        m = product(lambda c, d, k: ld_ref[c, d, k], gn_ref, [[None, None] for _ in range(3)])
        for d in range(2):
            i = 2 * p + d
            ur = gn_ref[0, i] + (m[0][d] - m[1][d])
            ui = gn_ref[1, i] + (m[2][d] - (m[0][d] + m[1][d]))
            out_ref[0, i] = ur.reshape(orb * atoms, energies).astype(BF16)
            out_ref[1, i] = ui.reshape(orb * atoms, energies).astype(BF16)
        sent(p).start()
        return carry

    lax.fori_loop(0, orb // 2, pair, 0, unroll=1)
    for p in range(orb // 2):
        sent(p).wait()


def move(value, axis, target):
    count = lax.axis_size(axis)
    return lax.ppermute(value, axis, [(i, target(i) % count) for i in range(count)])


def pair(i):
    return i ^ 1


def cross(i):
    return i + 1 if i & 1 else i - 1


def relay(i, count):
    if i & 1:
        return i - 2 if i > 1 else 0
    return i + 2 if i + 2 < count else count - 1


def move_far(value):
    atoms, energies = lax.axis_size("atom"), lax.axis_size("energy")
    moves = []
    for a in range(atoms):
        b = a + 1 if a & 1 else a - 1
        for e in range(energies):
            target = (b, e) if 0 <= b < atoms else (a, (e ^ 1) % energies)
            moves.append((a * energies + e, target[0] * energies + target[1]))
    return lax.ppermute(value, ("atom", "energy"), moves)


def per_device(bare_green, coupling_grad, neighbours, shifts, strength, occupation):
    _, orb, _, atoms, energies = bare_green.shape
    bonds = coupling_grad.shape[0]
    rows = orb * orb * atoms
    span = orb * atoms
    cols = -(-rows // LANES) * LANES
    period = span * LANES // math.gcd(span, LANES)
    early = orb // 3
    late = 2 * (orb - early) * span + 2 * span
    vmem = pl.BlockSpec(memory_space=pltpu.VMEM)
    smem = pl.BlockSpec(memory_space=pltpu.SMEM)
    small = pltpu.CompilerParams(vmem_limit_bytes=20 * 1024 * 1024)

    def shape(*dims, kind=BF16):
        return jax.ShapeDtypeStruct(dims, kind)

    def call(kernel, name, out_shape, *operands, scratch=(), scalars=()):
        return pl.pallas_call(
            kernel, out_shape=out_shape, name=name,
            in_specs=[smem if i in scalars else vmem for i in range(len(operands))],
            out_specs=jax.tree.map(lambda _: vmem, out_shape),
            scratch_shapes=scratch, compiler_params=small,
        )(*operands)

    green = bare_green.reshape(2, rows, energies)
    near = move(green, "atom", pair)
    grads = jnp.transpose(coupling_grad, (0, 1, 3, 2)).reshape(bonds * orb * atoms, orb)
    phonons = [x[None] for x in (shifts, strength, occupation)]
    fetched = [pltpu.with_memory_space_constraint(x, pltpu.HBM) for x in (green, grads, neighbours, *phonons)]
    edge, held, grads, near_atoms, *phonons = pl.pallas_call(
        functools.partial(pack_kernel, orb), name="pack",
        out_shape=[shape(2 * span, LANES), shape(2, rows, energies), shape(*grads.shape),
                   shape(bonds, 16, LANES, kind=jnp.int32)] + [shape(*x.shape, kind=x.dtype) for x in phonons],
        in_specs=[pl.BlockSpec(memory_space=pltpu.HBM)] * 6, out_specs=[vmem] * 7,
        scratch_shapes=[pltpu.SMEM(neighbours.shape, jnp.int32), pltpu.SemaphoreType.DMA((6,))],
        compiler_params=small,
    )(*fetched)
    left, right, table = call(
        functools.partial(factors_kernel, orb, atoms), "factors",
        [shape(bonds, orb, 16, cols), shape(3, bonds, span // 16, 16, period),
         shape(orb, energies + LANES, energies)],
        grads, near_atoms, *phonons)
    weight = shape(orb, span, cols)
    plain = shape(3, orb, span // 8, 8, energies, kind=F32)
    w_near, w_own, gn, gd = call(
        functools.partial(weights_kernel, orb, atoms), "weights",
        [weight, weight, plain, shape(3, orb, orb, 8, energies, kind=F32)], left, right, held)
    join, rim = call(
        join_kernel, "join", [shape(late, energies), shape(2 * span, LANES)],
        move(edge, "energy", pair), move(edge, "energy", cross), held, w_near)
    far_join = move_far(join)
    w_far = call(far_kernel, "far_weights", weight, left, right, join)
    passed, near_edge = call(
        functools.partial(pass_kernel, orb), "pack_near",
        [shape(2, early * span, energies), shape(2 * span, LANES)], near, w_far)
    far_first = move(passed, "atom", lambda i: relay(i, lax.axis_size("atom")))
    own = call(
        functools.partial(own_kernel, orb), "own", shape(rows, 2 * energies, kind=F32), table, held, rim, w_own)

    result = pl.pallas_call(
        functools.partial(final_kernel, orb, atoms), name="green_update",
        out_shape=shape(2, orb, span, energies),
        in_specs=[vmem] * 11, out_specs=pl.BlockSpec(memory_space=pltpu.HBM),
        scratch_shapes=[
            pltpu.VMEM(plain.shape, F32), pltpu.VMEM((3, 2, orb, 8, energies), F32),
            pltpu.VMEM((2, orb, span, energies), BF16), pltpu.SemaphoreType.DMA((orb // 2,))],
        compiler_params=small,
    )(near, move(near_edge, "energy", pair), move(near_edge, "energy", cross), far_first, far_join, w_near, w_far, own, table, gn, gd)
    return result.reshape(bare_green.shape)


def solution(mesh):
    placed = (
        P(None, None, None, "atom", "energy"),
        P(None, None, None, "atom"),
        P("atom", None),
        P(),
        P(),
        P(),
    )
    return jax.shard_map(
        per_device,
        mesh=mesh,
        in_specs=placed,
        out_specs=P(None, None, None, "atom", "energy"),
        check_vma=False,
    )
```

```python
import functools
import math
import jax
import jax.numpy as jnp
from jax import lax
from jax.experimental import pallas as pl
from jax.experimental.pallas import tpu as pltpu
from jax.sharding import PartitionSpec as P

WIDTH = 4
EDGE = 2 * WIDTH
LANES = 128
F32 = jnp.float32
BF16 = jnp.bfloat16


def iota(shape, axis):
    return lax.broadcasted_iota(jnp.int32, shape, axis)


def dot(a, b, dims=((1,), (0,))):
    return lax.dot_general(a, b, (dims, ((), ())), preferred_element_type=F32)


def steps_below(x, step, most):
    return sum((x >= step * m).astype(jnp.int32) for m in range(1, most))


def pack_edges(orb, g_ref, edge_ref):
    span = g_ref.shape[1] // orb
    lane = iota((span, LANES), 1)
    for r in range(2):
        total = jnp.zeros((span, LANES), F32)
        for k in range(orb):
            x = g_ref[r, k * span:(k + 1) * span].astype(F32)
            turned = pltpu.roll(x, EDGE * k + WIDTH, 1)
            total = jnp.where((lane >= EDGE * k) & (lane < EDGE * (k + 1)), turned, total)
        edge_ref[r * span:(r + 1) * span] = total.astype(BF16)


def from_sides(pair_ref, cross_ref):
    below = ((iota(pair_ref.shape, 1) & WIDTH) == 0) ^ ((lax.axis_index("energy") & 1) == 0)
    return jnp.where(below, pair_ref[...].astype(F32), cross_ref[...].astype(F32)).astype(BF16)


def pack_kernel(orb, g_hbm, c_hbm, nbr_hbm, sh_hbm, st_hbm, oc_hbm,
                edge_ref, g_ref, c_ref, near_ref, sh_ref, st_ref, oc_ref, nbr_ref, sems):
    ends = ((g_hbm, g_ref), (nbr_hbm, nbr_ref), (c_hbm, c_ref), (sh_hbm, sh_ref), (st_hbm, st_ref), (oc_hbm, oc_ref))
    copies = [pltpu.make_async_copy(source, target, sems.at[i]) for i, (source, target) in enumerate(ends)]
    for copy in copies:
        copy.start()
    copies[0].wait()
    pack_edges(orb, g_ref, edge_ref)
    copies[1].wait()
    atoms, bonds = nbr_ref.shape
    own = iota(near_ref.shape[1:], 0) & (atoms - 1)
    for n in range(bonds):
        near = jnp.zeros(near_ref.shape[1:], jnp.int32)
        for a in range(atoms):
            near = jnp.where(own == a, nbr_ref[a, n], near)
        near_ref[n] = near
    for copy in copies[2:]:
        copy.wait()


def join_kernel(pair_ref, cross_ref, g_ref, after_ref, out_ref, rim_ref):
    rows = g_ref.shape[1]
    rim = pair_ref.shape[0]
    rest = (out_ref.shape[0] - rim) // 2
    for r in range(2):
        out_ref[r * rest:(r + 1) * rest] = g_ref[r, rows - rest:]
    halo = from_sides(pair_ref, cross_ref)
    out_ref[2 * rest:] = halo
    rim_ref[...] = halo


def pass_kernel(x_ref, after_ref, out_ref):
    out_ref[...] = x_ref[:, :out_ref.shape[1]]


def band_weights(sh_ref, st_ref, oc_ref):
    shifts = sh_ref[...]
    emit = st_ref[...] * oc_ref[...]
    absorb = st_ref[...] * (oc_ref[...] + 1.0)
    zero = jnp.zeros_like(emit)
    weights = []
    for o in range(-WIDTH, WIDTH + 1):
        both = jnp.where(shifts == -o, emit, zero) + jnp.where(shifts == o, absorb, zero)
        weights.append(jnp.sum(both, axis=1, keepdims=True))
    return weights


def banded(weights, gap, keep=None):
    table = jnp.zeros(gap.shape, F32)
    for o in range(-WIDTH, WIDTH + 1):
        hit = gap == o
        if keep is not None:
            hit = hit & keep
        table = jnp.where(hit, weights[o + WIDTH], table)
    return table.astype(BF16)


def factors_kernel(orb, atoms, c_ref, near_ref, sh_ref, st_ref, oc_ref, t1_ref, t2_ref, table_ref):
    bonds = near_ref.shape[0]
    energies = table_ref.shape[2]
    span = orb * atoms
    cols = t1_ref.shape[3]
    period = t2_ref.shape[4]
    here = lax.axis_index("atom")
    place = lax.axis_index("energy")
    last = lax.axis_size("energy") - 1

    weights = band_weights(sh_ref, st_ref, oc_ref)
    band = banded(weights, iota((energies, energies), 0) - iota((energies, energies), 1))
    rim = (LANES, energies)
    row = iota(rim, 0)
    spot = row & (EDGE - 1)
    below = spot < WIDTH
    keep = jnp.where(below, jnp.where(place > 0, 1, 0), jnp.where(place < last, 1, 0)) > 0
    edge = banded(weights, jnp.where(below, spot - WIDTH, spot - WIDTH + energies) - iota(rim, 1), keep)
    for k in range(orb):
        table_ref[k, :energies] = band
        table_ref[k, energies:] = jnp.where((row >= EDGE * k) & (row < EDGE * (k + 1)), edge, jnp.zeros_like(edge))

    c = c_ref[...]
    krow, klane = iota((orb, cols), 0), iota((orb, cols), 1)
    spread = ((klane >= krow * span) & (klane < (krow + 1) * span)).astype(F32).astype(BF16)
    left = dot(c, spread).reshape(bonds * orb * atoms // 8, 8, cols)
    turned = pltpu.roll(left, atoms, 1)
    upper = iota(left.shape, 1) < atoms
    first = jnp.where(upper, left, turned)
    second = jnp.where(upper, turned, left)
    both = jnp.stack([first, second], axis=1).reshape(bonds, orb, 8, cols)
    t1_ref[...] = jnp.concatenate([both, both], axis=2).astype(BF16)

    lrow, llane = iota((orb, period), 0), iota((orb, period), 1)
    inner = llane - span * steps_below(llane, span, period // span)
    spread = ((inner >= lrow * atoms) & (inner < (lrow + 1) * atoms)).astype(F32).astype(BF16)
    right = dot(c, spread).reshape(bonds, span // 16, 16, period)
    odd = here & 1
    base = (here + 1 - 2 * odd, here, here - 1 + 2 * odd)
    other = iota((16, period), 1) & (atoms - 1)
    for n in range(bonds):
        near = jnp.concatenate([near_ref[n]] * (period // LANES), axis=1)
        for s in range(3):
            mask = near == other + base[s] * atoms
            t2_ref[s, n] = jnp.where(mask[None], right[n], 0.0).astype(BF16)


def weights_kernel(orb, atoms, t1_ref, t2_ref, g_ref, wn_ref, wo_ref, gn_ref, gd_ref):
    gr = g_ref[0].astype(F32)
    gi = g_ref[1].astype(F32)
    for c, x in enumerate((gr, gi, gr + gi)):
        gn_ref[c] = x.reshape(gn_ref.shape[1:])
        gd_ref[c] = doubled(x, orb, atoms)
    fill(t1_ref, t2_ref, (wn_ref, wo_ref), 0)


def far_kernel(t1_ref, t2_ref, after_ref, wf_ref):
    fill(t1_ref, t2_ref, (wf_ref,), 2)


def own_kernel(orb, table_ref, g_ref, rim_ref, wo_ref, s_ref):
    s_ref[...] = slab_products([wo_ref], [whole(g_ref, orb)], [rim_ref[...]], table_ref)


def fill(t1_ref, t2_ref, outs, first):
    bonds, orb = t1_ref.shape[:2]
    groups, period = t2_ref.shape[2], t2_ref.shape[4]
    for t in range(t1_ref.shape[3] // LANES):
        at = slice(t * LANES, (t + 1) * LANES)
        start = (t * LANES) % period
        cut = slice(start, start + LANES)
        for s, out in enumerate(outs):
            held = [[t2_ref[s + first, n, q, :, cut] for n in range(bonds)] for q in range(groups)]

            def body(i, carry):
                x = [t1_ref[n, i, :, at] for n in range(bonds)]
                for q in range(groups):
                    terms = [x[n] * held[q][n] for n in range(bonds)]
                    while len(terms) > 1:
                        pairs = [terms[n] + terms[n + 1] for n in range(0, len(terms) - 1, 2)]
                        terms = pairs + terms[2 * len(pairs):]
                    out[i, q * 16:(q + 1) * 16, at] = terms[0]
                return carry

            lax.fori_loop(0, orb, body, 0, unroll=orb)


def rim_of(join_ref, span):
    return join_ref[join_ref.shape[0] - 2 * span:]


def whole(ref, orb):
    return [[(ref.at[0], k), (ref.at[1], k)] for k in range(orb)]


def joined(parts, join_ref, orb, span):
    blocks = []
    for ref in parts:
        blocks += [[(ref.at[0], k), (ref.at[1], k)] for k in range(ref.shape[1] // span)]
    late = orb - len(blocks)
    return blocks + [[(join_ref, k), (join_ref, late + k)] for k in range(late)]


def slab_products(w_refs, slabs, rims, table_ref):
    orb = len(slabs[0])
    span = rims[0].shape[0] // 2
    rims = jnp.concatenate(rims, axis=0)
    summed = []
    for k in range(orb):
        body = jnp.concatenate([ref[i * span:(i + 1) * span] for slab in slabs for ref, i in slab[k]], axis=0)
        summed.append(dot(jnp.concatenate([body, rims], axis=1), table_ref[k]).astype(BF16))
    total = None
    for s, w_ref in enumerate(w_refs):
        at = 2 * s * span
        right = jnp.concatenate(
            [jnp.concatenate([x[at:at + span], x[at + span:at + 2 * span]], axis=1) for x in summed], axis=0)
        rows = right.shape[0]
        w = w_ref[...].reshape(rows, w_ref.shape[2])[:, :rows]
        part = dot(w, right)
        total = part if total is None else total + part
    return total


def doubled(x, orb, atoms):
    pairs = x.reshape(orb * orb * atoms // 8, 8, x.shape[1])
    turned = pltpu.roll(pairs, atoms, 1)
    upper = iota(pairs.shape, 1) < atoms
    first = jnp.where(upper, pairs, turned)
    second = jnp.where(upper, turned, pairs)
    return jnp.stack([first, second], axis=1).reshape(orb, orb, 8, x.shape[1])


def final_kernel(orb, atoms, near_ref, pair_ref, cross_ref, ff_ref, fj_ref, wn_ref, wf_ref, s_ref, table_ref, gn_ref, gd_ref,
                 out_hbm, sn_ref, ld_ref, out_ref, sems):
    energies = table_ref.shape[2]
    span = orb * atoms
    groups = span // 8
    slabs = [whole(near_ref, orb), joined((ff_ref,), fj_ref, orb, span)]
    rims = [from_sides(pair_ref, cross_ref), rim_of(fj_ref, span)]
    total = s_ref[...] + slab_products([wn_ref, wf_ref], slabs, rims, table_ref)
    re, im = total[:, :energies], total[:, energies:]
    for c, x in enumerate((re, im, re + im)):
        sn_ref[c] = x.reshape(orb, groups, 8, energies)

    def product(left, right_ref, acc):
        for k in range(orb):
            for c in range(3):
                right = right_ref[c, k]
                for d in range(2):
                    term = left(c, d, k)[None] * right
                    acc[c][d] = term if acc[c][d] is None else acc[c][d] + term
        return acc

    def sent(p):
        at = pl.ds(2 * p, 2)
        return pltpu.make_async_copy(out_ref.at[:, at], out_hbm.at[:, at], sems.at[p])

    def pair(p, carry):
        m = product(lambda c, d, k: gd_ref[c, 2 * p + d, k], sn_ref, [[None, None] for _ in range(3)])
        upper = iota((groups, 8, energies), 1) < atoms
        for d in range(2):
            lr = m[0][d] - m[1][d]
            li = m[2][d] - (m[0][d] + m[1][d])
            rows = []
            for x in (lr, li):
                turned = pltpu.roll(x, atoms, 1)
                first = jnp.where(upper, x, turned)
                second = jnp.where(upper, turned, x)
                rows.append(jnp.stack([first, second], axis=1).reshape(orb, 8, energies))
            for c, x in enumerate((rows[0], rows[1], rows[0] + rows[1])):
                ld_ref[c, d] = x
        m = product(lambda c, d, k: ld_ref[c, d, k], gn_ref, [[None, None] for _ in range(3)])
        for d in range(2):
            i = 2 * p + d
            ur = gn_ref[0, i] + (m[0][d] - m[1][d])
            ui = gn_ref[1, i] + (m[2][d] - (m[0][d] + m[1][d]))
            out_ref[0, i] = ur.reshape(orb * atoms, energies).astype(BF16)
            out_ref[1, i] = ui.reshape(orb * atoms, energies).astype(BF16)
        sent(p).start()
        return carry

    lax.fori_loop(0, orb // 2, pair, 0, unroll=1)
    for p in range(orb // 2):
        sent(p).wait()


def move(value, axis, target):
    count = lax.axis_size(axis)
    return lax.ppermute(value, axis, [(i, target(i) % count) for i in range(count)])


def pair(i):
    return i ^ 1


def cross(i):
    return i + 1 if i & 1 else i - 1


def relay(i, count):
    if i & 1:
        return i - 2 if i > 1 else 0
    return i + 2 if i + 2 < count else count - 1


def move_far(value):
    atoms, energies = lax.axis_size("atom"), lax.axis_size("energy")
    moves = []
    for a in range(atoms):
        b = a + 1 if a & 1 else a - 1
        for e in range(energies):
            target = (b, e) if 0 <= b < atoms else (a, (e ^ 1) % energies)
            moves.append((a * energies + e, target[0] * energies + target[1]))
    return lax.ppermute(value, ("atom", "energy"), moves)


def per_device(bare_green, coupling_grad, neighbours, shifts, strength, occupation):
    _, orb, _, atoms, energies = bare_green.shape
    bonds = coupling_grad.shape[0]
    rows = orb * orb * atoms
    span = orb * atoms
    cols = -(-rows // LANES) * LANES
    period = span * LANES // math.gcd(span, LANES)
    early = orb // 3
    late = 2 * (orb - early) * span + 2 * span
    vmem = pl.BlockSpec(memory_space=pltpu.VMEM)
    smem = pl.BlockSpec(memory_space=pltpu.SMEM)
    small = pltpu.CompilerParams(vmem_limit_bytes=20 * 1024 * 1024)

    def shape(*dims, kind=BF16):
        return jax.ShapeDtypeStruct(dims, kind)

    def call(kernel, name, out_shape, *operands, scratch=(), scalars=()):
        return pl.pallas_call(
            kernel, out_shape=out_shape, name=name,
            in_specs=[smem if i in scalars else vmem for i in range(len(operands))],
            out_specs=jax.tree.map(lambda _: vmem, out_shape),
            scratch_shapes=scratch, compiler_params=small,
        )(*operands)

    green = bare_green.reshape(2, rows, energies)
    near = move(green, "atom", pair)
    grads = jnp.transpose(coupling_grad, (0, 1, 3, 2)).reshape(bonds * orb * atoms, orb)
    phonons = [x[None] for x in (shifts, strength, occupation)]
    fetched = [pltpu.with_memory_space_constraint(x, pltpu.HBM) for x in (green, grads, neighbours, *phonons)]
    edge, held, grads, near_atoms, *phonons = pl.pallas_call(
        functools.partial(pack_kernel, orb), name="pack",
        out_shape=[shape(2 * span, LANES), shape(2, rows, energies), shape(*grads.shape),
                   shape(bonds, 16, LANES, kind=jnp.int32)] + [shape(*x.shape, kind=x.dtype) for x in phonons],
        in_specs=[pl.BlockSpec(memory_space=pltpu.HBM)] * 6, out_specs=[vmem] * 7,
        scratch_shapes=[pltpu.SMEM(neighbours.shape, jnp.int32), pltpu.SemaphoreType.DMA((6,))],
        compiler_params=small,
    )(*fetched)
    left, right, table = call(
        functools.partial(factors_kernel, orb, atoms), "factors",
        [shape(bonds, orb, 16, cols), shape(3, bonds, span // 16, 16, period),
         shape(orb, energies + LANES, energies)],
        grads, near_atoms, *phonons)
    weight = shape(orb, span, cols)
    plain = shape(3, orb, span // 8, 8, energies, kind=F32)
    w_near, w_own, gn, gd = call(
        functools.partial(weights_kernel, orb, atoms), "weights",
        [weight, weight, plain, shape(3, orb, orb, 8, energies, kind=F32)], left, right, held)
    join, rim = call(
        join_kernel, "join", [shape(late, energies), shape(2 * span, LANES)],
        move(edge, "energy", pair), move(edge, "energy", cross), held, w_near)
    far_join = move_far(join)
    w_far = call(far_kernel, "far_weights", weight, left, right, join)
    passed = call(pass_kernel, "pass", shape(2, early * span, energies), near, w_far)
    near_edge = call(functools.partial(pack_edges, orb), "pack_near", shape(2 * span, LANES), near)
    far_first = move(passed, "atom", lambda i: relay(i, lax.axis_size("atom")))
    own = call(
        functools.partial(own_kernel, orb), "own", shape(rows, 2 * energies, kind=F32), table, held, rim, w_own)

    result = pl.pallas_call(
        functools.partial(final_kernel, orb, atoms), name="green_update",
        out_shape=shape(2, orb, span, energies),
        in_specs=[vmem] * 11, out_specs=pl.BlockSpec(memory_space=pltpu.HBM),
        scratch_shapes=[
            pltpu.VMEM(plain.shape, F32), pltpu.VMEM((3, 2, orb, 8, energies), F32),
            pltpu.VMEM((2, orb, span, energies), BF16), pltpu.SemaphoreType.DMA((orb // 2,))],
        compiler_params=small,
    )(near, move(near_edge, "energy", pair), move(near_edge, "energy", cross), far_first, far_join, w_near, w_far, own, table, gn, gd)
    return result.reshape(bare_green.shape)


def solution(mesh):
    placed = (
        P(None, None, None, "atom", "energy"),
        P(None, None, None, "atom"),
        P("atom", None),
        P(),
        P(),
        P(),
    )
    return jax.shard_map(
        per_device,
        mesh=mesh,
        in_specs=placed,
        out_specs=P(None, None, None, "atom", "energy"),
        check_vma=False,
    )
```
